32 devices in a mesh: img: 2 (over y), gx: 4 (over z), gy: 4 (over x, core).
Axes of the slice: x: 2, y: 2, z: 4, core: 2. Of those that a mesh axis runs over, the one named last changes fastest.
Arguments:
- conc_old: float32 [128, 64, 128], P(('img', 'gx'), 'gy'), parts along dimension 0, may hold values from -1 to 1
- chem_old: float32 [128, 64, 128], P(('img', 'gx'), 'gy'), parts along dimension 0, may hold values from -4 to 4
Outputs:
- conc_new: float32 [128, 64, 128], P(('img', 'gx'), 'gy'), parts along dimension 0
- chem_new: float32 [128, 64, 128], P(('img', 'gx'), 'gy'), parts along dimension 0
The draws below stay inside these ranges and needn't reach their ends.
There are 2 independent parts, one for each index of `img`. The reference program is written for one: setup_inputs(seed, part) draws one part's arguments, and reference() takes and returns one part's arrays. A program takes and returns all parts, laid end to end along the dimension named above; each array names one. Nothing has to cross between parts.
All inputs are finite; a program needn't handle non-finite values.
Results may differ from the reference program's by a relative error of at most 0.0001.
Values sent between devices are 32-bit elements; how exact they have to be, the bound alone decides.
A program may use at most 128 MiB of HBM per device.

```python
import jax
import jax.numpy as jnp

LEVELS = 4
SWEEPS = 2
COARSE = 6
NX = 64
NY = 64
NZ = 128


def shard_levels(stream_key, extent, pieces, smallest, largest):
    gain = 1.0
    for axis_at, parts in pieces:
        heights = jax.random.uniform(jax.random.fold_in(jax.random.fold_in(stream_key, 6), axis_at), (parts,), jnp.float32, smallest / len(pieces), largest / len(pieces))
        gain = gain * jnp.repeat(jnp.exp(heights), extent[axis_at] // parts).reshape((-1,) + (1,) * (len(extent) - 1 - axis_at))
    return gain


def bell_draw(own_key, extent, scale, limit, cuts=(), kind=jnp.bfloat16):
    drawn = jax.random.normal(own_key, extent, jnp.float32) * scale
    if len(cuts) > 0:
        drawn = shard_levels(own_key, extent, cuts, -0.22, 0.18) * drawn
    return jnp.clip(drawn, min=-limit, max=limit).astype(kind)


def setup_inputs(seed: int = 0, part: int = 0) -> dict:
    keys = jax.random.split(jax.random.key(seed), 3)
    own_keys = jax.random.split(jax.random.fold_in(keys[2], part), 3)
    conc_old = jnp.clip(jax.random.uniform(own_keys[0], (NX, NY, NZ), jnp.float32, -1.0, 1.0) * shard_levels(own_keys[0], (NX, NY, NZ), ((0, 4), (1, 4)), -0.4, 0.0), -1.0, 1.0)
    chem_old = bell_draw(own_keys[1], (NX, NY, NZ), 1.0, 4.0, ((0, 4), (1, 4)), jnp.float32)
    return dict(conc_old=conc_old, chem_old=chem_old)


TIME_STEP = 32.0
GRADIENT_ENERGY = 0.5
STABILIZER = 2.0
DAMPING = 0.7


def face_weights(mob_padded, level_scale):
    middle = mob_padded[1:-1, 1:-1, :]
    half_scale = 0.5 * level_scale
    weights = (half_scale * (middle + mob_padded[2:, 1:-1, :]),
               half_scale * (middle + mob_padded[:-2, 1:-1, :]),
               half_scale * (middle + mob_padded[1:-1, 2:, :]),
               half_scale * (middle + mob_padded[1:-1, :-2, :]),
               half_scale * (middle + jnp.roll(middle, -1, axis=2)),
               half_scale * (middle + jnp.roll(middle, 1, axis=2)))
    total_weight = weights[0] + weights[1] + weights[2] + weights[3] + weights[4] + weights[5]
    return weights, total_weight


def neighbour_list(padded, middle):
    return (padded[2:, 1:-1, :], padded[:-2, 1:-1, :], padded[1:-1, 2:, :], padded[1:-1, :-2, :],
            jnp.roll(middle, -1, axis=2), jnp.roll(middle, 1, axis=2))


def apply_operator(padded, weights, level_scale):
    middle = padded[:, 1:-1, 1:-1, :]
    conc_near = neighbour_list(padded[0], middle[0])
    chem_near = neighbour_list(padded[1], middle[1])
    flux = weights[0] * (chem_near[0] - middle[1])
    for position in range(1, 6):
        flux = flux + weights[position] * (chem_near[position] - middle[1])
    laplace = conc_near[0] + conc_near[1] + conc_near[2] + conc_near[3] + conc_near[4] + conc_near[5] - 6.0 * middle[0]
    first_eq = middle[0] - TIME_STEP * flux
    second_eq = middle[1] - STABILIZER * middle[0] + GRADIENT_ENERGY * level_scale * laplace
    return jnp.stack([first_eq, second_eq])


def update(residual, total_weight, level_scale):
    diagonal = STABILIZER + 6.0 * GRADIENT_ENERGY * level_scale
    coupling = TIME_STEP * total_weight
    determinant = 1.0 + coupling * diagonal
    conc_step = (residual[0] - coupling * residual[1]) / determinant
    chem_step = (residual[1] + diagonal * residual[0]) / determinant
    return DAMPING * jnp.stack([conc_step, chem_step])


def sweep_once(padded, right_side, mob_padded, level_scale):
    weights, total_weight = face_weights(mob_padded, level_scale)
    residual = right_side - apply_operator(padded, weights, level_scale)
    return padded[:, 1:-1, 1:-1, :] + update(residual, total_weight, level_scale)


def defect(padded, right_side, mob_padded, level_scale):
    weights = face_weights(mob_padded, level_scale)[0]
    return right_side - apply_operator(padded, weights, level_scale)


def coarsen(values):
    dims_now = values.shape
    grouped = values.reshape(dims_now[:-3] + (dims_now[-3] // 2, 2, dims_now[-2] // 2, 2, dims_now[-1] // 2, 2))
    return jnp.sum(grouped, axis=(-5, -3, -1)) * 0.125


def refine(values):
    for axis_pos in (-3, -2, -1):
        values = jnp.repeat(values, 2, axis=axis_pos)
    return values


def wrap_fields(fields):
    return jnp.pad(fields, ((0, 0), (1, 1), (1, 1), (0, 0)), mode="wrap")


def wrap_cells(cells):
    return jnp.pad(cells, ((1, 1), (1, 1), (0, 0)), mode="wrap")


def reference(conc_old, chem_old):
    mobility = 0.1 + jnp.square(1.0 - conc_old * conc_old)
    level_data = []
    for level_index in range(LEVELS):
        level_data.append((wrap_cells(mobility), 0.25 ** level_index))
        if level_index + 1 < LEVELS:
            mobility = coarsen(mobility)

    def cycle_level(level_index, fields, right_side):
        mob_padded, level_scale = level_data[level_index]
        if level_index == LEVELS - 1:
            fields = jnp.zeros_like(right_side)
            for sweep_index in range(COARSE):
                fields = sweep_once(wrap_fields(fields), right_side, mob_padded, level_scale)
            return fields
        for sweep_index in range(SWEEPS):
            fields = sweep_once(wrap_fields(fields), right_side, mob_padded, level_scale)
        residual = defect(wrap_fields(fields), right_side, mob_padded, level_scale)
        coarse_right = coarsen(residual)
        correction = cycle_level(level_index + 1, jnp.zeros_like(coarse_right), coarse_right)
        fields = fields + refine(correction)
        for sweep_index in range(SWEEPS):
            fields = sweep_once(wrap_fields(fields), right_side, mob_padded, level_scale)
        return fields

    right_side = jnp.stack([conc_old, conc_old * conc_old * conc_old - (1.0 + STABILIZER) * conc_old])
    start_fields = jnp.stack([conc_old, chem_old])
    result = cycle_level(0, start_fields, right_side)
    return result[0], result[1]
```

```python
import functools

import jax
import jax.numpy as jnp
from jax import lax
from jax.experimental import pallas as pl
from jax.experimental.pallas import tpu as pltpu
from jax.sharding import PartitionSpec as P

LEVELS = 4
SWEEPS = 2
COARSE = 6


TIME_STEP = 32.0
GRADIENT_ENERGY = 0.5
STABILIZER = 2.0
DAMPING = 0.7


def extended(cells, sides, width):
    for axis, dim in sides:
        count = lax.axis_size(axis)
        head = lax.slice_in_dim(cells, 0, width, axis=dim)
        tail = lax.slice_in_dim(cells, cells.shape[dim] - width, cells.shape[dim], axis=dim)
        cells = jnp.concatenate(
            [
                lax.ppermute(tail, axis, [(i, (i + 1) % count) for i in range(count)]),
                cells,
                lax.ppermute(head, axis, [((i + 1) % count, i) for i in range(count)]),
            ],
            axis=dim,
        )
    return cells


def mobility_of(concentration):
    return 0.1 + jnp.square(1.0 - concentration * concentration)


def right_of(concentration):
    return jnp.stack(
        [
            concentration,
            concentration * concentration * concentration - (1.0 + STABILIZER) * concentration,
        ]
    )


def face_weights(mob_padded, level_scale):
    middle = mob_padded[1:-1, 1:-1, :]
    half_scale = 0.5 * level_scale
    weights = (
        half_scale * (middle + mob_padded[2:, 1:-1, :]),
        half_scale * (middle + mob_padded[:-2, 1:-1, :]),
        half_scale * (middle + mob_padded[1:-1, 2:, :]),
        half_scale * (middle + mob_padded[1:-1, :-2, :]),
        half_scale * (middle + jnp.roll(middle, -1, axis=2)),
        half_scale * (middle + jnp.roll(middle, 1, axis=2)),
    )
    total_weight = weights[0] + weights[1] + weights[2] + weights[3] + weights[4] + weights[5]
    return (weights, total_weight)


def neighbour_list(padded, middle):
    return (
        padded[2:, 1:-1, :],
        padded[:-2, 1:-1, :],
        padded[1:-1, 2:, :],
        padded[1:-1, :-2, :],
        jnp.roll(middle, -1, axis=2),
        jnp.roll(middle, 1, axis=2),
    )


def apply_operator(padded, weights, level_scale):
    middle = padded[:, 1:-1, 1:-1, :]
    conc_near = neighbour_list(padded[0], middle[0])
    chem_near = neighbour_list(padded[1], middle[1])
    flux = weights[0] * (chem_near[0] - middle[1])
    for position in range(1, 6):
        flux = flux + weights[position] * (chem_near[position] - middle[1])
    laplace = (
        conc_near[0]
        + conc_near[1]
        + conc_near[2]
        + conc_near[3]
        + conc_near[4]
        + conc_near[5]
        - 6.0 * middle[0]
    )
    first_eq = middle[0] - TIME_STEP * flux
    second_eq = middle[1] - STABILIZER * middle[0] + GRADIENT_ENERGY * level_scale * laplace
    return jnp.stack([first_eq, second_eq])


def update(residual, total_weight, level_scale):
    diagonal = STABILIZER + 6.0 * GRADIENT_ENERGY * level_scale
    coupling = TIME_STEP * total_weight
    determinant = 1.0 + coupling * diagonal
    conc_step = (residual[0] - coupling * residual[1]) / determinant
    chem_step = (residual[1] + diagonal * residual[0]) / determinant
    return DAMPING * jnp.stack([conc_step, chem_step])


def sweep_once(padded, right_side, mob_padded, level_scale):
    weights, total_weight = face_weights(mob_padded, level_scale)
    residual = right_side - apply_operator(padded, weights, level_scale)
    return padded[:, 1:-1, 1:-1, :] + update(residual, total_weight, level_scale)


def defect(padded, right_side, mob_padded, level_scale):
    weights = face_weights(mob_padded, level_scale)[0]
    return right_side - apply_operator(padded, weights, level_scale)


def coarsen(values):
    dims_now = values.shape
    grouped = values.reshape(
        dims_now[:-3] + (dims_now[-3] // 2, 2, dims_now[-2] // 2, 2, dims_now[-1] // 2, 2)
    )
    return jnp.sum(grouped, axis=(-5, -3, -1)) * 0.125


def refine(values):
    for axis_pos in (-3, -2, -1):
        values = jnp.repeat(values, 2, axis=axis_pos)
    return values


def trim_rim(values, width):
    return values[..., width:-width, width:-width, :]


def field_rim(fields):
    return extended(fields, (("gx", 1), ("gy", 2)), 1)


def coarsest_solve(right_side, mobility, level_scale):
    mob_padded = extended(mobility, (("gx", 0), ("gy", 1)), 1)
    fields = update(right_side, face_weights(mob_padded, level_scale)[1], level_scale)
    for sweep_index in range(COARSE - 1):
        padded = extended(fields, (("gx", 1), ("gy", 2)), 1)
        fields = sweep_once(padded, right_side, mob_padded, level_scale)
    return fields


def plain_solve(start_fields):
    outer_fields = field_rim(start_fields)
    mob_outer = mobility_of(outer_fields[0])
    mobility = trim_rim(mob_outer, 1)
    level_data = []
    for level_index in range(LEVELS - 1):
        if level_index == 0:
            mob_padded = mob_outer
        else:
            mob_padded = extended(mobility, (("gx", 0), ("gy", 1)), 1)
        level_data.append((mob_padded, 0.25**level_index))
        mobility = coarsen(mobility)
    coarsest_scale = 0.25 ** (LEVELS - 1)

    def cycle_level(level_index, right_side):
        if level_index == LEVELS - 1:
            return coarsest_solve(right_side, mobility, coarsest_scale)
        mob_padded, level_scale = level_data[level_index]
        if level_index == 0:
            fields = sweep_once(outer_fields, right_side, mob_padded, level_scale)
        else:
            fields = update(right_side, face_weights(mob_padded, level_scale)[1], level_scale)
        fields = sweep_once(field_rim(fields), right_side, mob_padded, level_scale)
        residual = defect(field_rim(fields), right_side, mob_padded, level_scale)
        fields = fields + refine(cycle_level(level_index + 1, coarsen(residual)))
        for sweep_index in range(SWEEPS):
            fields = sweep_once(field_rim(fields), right_side, mob_padded, level_scale)
        return fields

    return cycle_level(0, right_of(start_fields[0]))


MESH = pl.DeviceIdType.MESH
HALO = 4
SIDES = (("lo", -1), ("hi", 1))
CORNERS = ((-1, -1), (-1, 1), (1, -1), (1, 1))


def iota(shape, dim):
    return lax.broadcasted_iota(jnp.int32, shape, dim)


def turn(values, shift, axis):
    size = values.shape[axis]
    return pltpu.roll(values, shift % size, axis)


def near_sum(values, row_step, lane_step, wrap=False):
    if wrap:
        middle = values
        total = jnp.concatenate([values[1:], values[:1]], 0) + jnp.concatenate(
            [values[-1:], values[:-1]], 0
        )
    else:
        middle = values[1:-1]
        total = values[2:] + values[:-2]
    total = total + (turn(middle, row_step, 1) + turn(middle, -row_step, 1))
    return total + (turn(middle, lane_step, 2) + turn(middle, -lane_step, 2))


def pair_sum(values, step, axis):
    low = (iota(values.shape, axis) // step) % 2 == 0
    return values + jnp.where(low, turn(values, -step, axis), turn(values, step, axis))


def pair_rows(values):
    grouped = values.reshape((values.shape[0] // 2, 2) + values.shape[1:])
    return grouped[:, 0] + grouped[:, 1]


def twice(values):
    return jnp.concatenate([values[i // 2 : i // 2 + 1] for i in range(2 * values.shape[0])], 0)


class Level:
    def __init__(self, scale, mob, mob_sum, row_step, lane_step, wrap=False):
        self.scale, self.mob = scale, mob
        self.row_step, self.lane_step, self.wrap = row_step, lane_step, wrap
        self.half = 0.5 * TIME_STEP * scale
        self.diagonal = STABILIZER + 6.0 * GRADIENT_ENERGY * scale
        self.coupling = self.half * (6.0 * mob + mob_sum)
        self.damp = DAMPING / (1.0 + self.coupling * self.diagonal)

    def part(self, values, size):
        off = (values.shape[0] - size) // 2
        return values[off : off + size]

    def residual(self, conc, chem, right):
        size = conc.shape[0] if self.wrap else conc.shape[0] - 2
        sums = functools.partial(
            near_sum, row_step=self.row_step, lane_step=self.lane_step, wrap=self.wrap
        )
        carried = self.part(self.mob, conc.shape[0]) * chem
        mob = self.part(self.mob, size)
        c, u = self.part(conc, size), self.part(chem, size)
        first = (
            self.part(right[0], size)
            - c
            + self.half * (mob * sums(chem) + sums(carried))
            - self.part(self.coupling, size) * u
        )
        near = sums(conc) - 6.0 * c
        second = (
            self.part(right[1], size)
            - u
            + STABILIZER * c
            - (GRADIENT_ENERGY * self.scale) * near
        )
        return first, second

    def step(self, first, second):
        size = first.shape[0]
        damp = self.part(self.damp, size)
        coupling = self.part(self.coupling, size)
        return damp * (first - coupling * second), damp * (second + self.diagonal * first)

    def sweep(self, conc, chem, right):
        first, second = self.residual(conc, chem, right)
        size = first.shape[0]
        dc, du = self.step(first, second)
        return self.part(conc, size) + dc, self.part(chem, size) + du


def split_halves(first, second, first_high, second_high):
    low = iota(first.shape, 1) < 4
    first = turn(first, 4, 1) if first_high else first
    second = second if second_high else turn(second, 4, 1)
    return jnp.where(low, first, second)


def cycle_kernel(nx, ny, conc_ref, chem_ref, conc_out, chem_out, *scratch):
    (
        edge0,
        from_x0,
        from_y0,
        from_d0,
        edge1,
        whole1,
        from_x1,
        from_y1,
        from_d1,
        pack2,
        grid2,
        rows_buf,
        send_sem,
        recv_sem,
    ) = scratch
    img, gx, gy = lax.axis_index("img"), lax.axis_index("gx"), lax.axis_index("gy")

    def at(dx, dy):
        return (img, lax.rem(gx + dx + nx, nx), lax.rem(gy + dy + ny, ny))

    peers = [(dx, dy) for dx in range(nx) for dy in range(ny) if (dx, dy) != (0, 0)]
    barrier = pltpu.get_barrier_semaphore()
    for dx, dy in peers:
        pl.semaphore_signal(barrier, inc=1, device_id=at(dx, dy), device_id_type=MESH)

    used = [0]
    started = []

    def send(src, dst, dx, dy):
        index = used[0]
        used[0] += 1
        copy = pltpu.make_async_remote_copy(
            src_ref=src,
            dst_ref=dst,
            send_sem=send_sem.at[index],
            recv_sem=recv_sem.at[index],
            device_id=at(dx, dy),
            device_id_type=MESH,
        )
        copy.start()
        started.append(copy)
        return copy

    size = conc_ref.shape[0]
    conc, chem = conc_ref[...], chem_ref[...]
    edge0[0] = split_halves(conc[:, :8], chem[:, :8], False, False)
    edge0[1] = split_halves(conc[:, -8:], chem[:, -8:], True, True)
    pl.semaphore_wait(barrier, len(peers))

    waits = []
    for side, dx in ((0, -1), (1, 1)):
        rows = pl.ds(0, HALO) if dx < 0 else pl.ds(size - HALO, HALO)
        waits.append(send(conc_ref.at[rows], from_x0.at[side, 0], dx, 0))
        waits.append(send(chem_ref.at[rows], from_x0.at[side, 1], dx, 0))
    for place, (dx, dy) in enumerate(CORNERS):
        rows = pl.ds(0, HALO - 1) if dx < 0 else pl.ds(size - HALO + 1, HALO - 1)
        waits.append(send(edge0.at[(dy + 1) // 2, rows], from_d0.at[place], dx, dy))
    for side, dy in ((0, -1), (1, 1)):
        waits.append(send(edge0.at[side], from_y0.at[side], 0, dy))
    for copy in waits:
        copy.wait_recv()

    def halo_rows(center, corners):
        lower, upper = corners[1], corners[0]
        return jnp.concatenate([lower[:1], lower, center, upper, upper[:1]], 0)

    def joined(right, left):
        low = iota(right.shape, 1) < 4
        return jnp.where(low, right, turn(left, 4, 1)), jnp.where(low, turn(right, 4, 1), left)

    right0 = halo_rows(from_y0[0], (from_d0[0], from_d0[2]))
    left0 = halo_rows(from_y0[1], (from_d0[1], from_d0[3]))
    conc_halo, chem_halo = joined(right0, left0)
    conc = jnp.concatenate([from_x0[1, 0], conc, from_x0[0, 0]], 0)
    chem = jnp.concatenate([from_x0[1, 1], chem, from_x0[0, 1]], 0)
    conc = jnp.concatenate([conc, conc_halo], 1)
    chem = jnp.concatenate([chem, chem_halo], 1)

    mob0 = mobility_of(conc)
    level0 = Level(1.0, mob0[1:-1], near_sum(mob0, 1, 1), 1, 1)
    level0.mob = mob0
    right_side0 = (conc, conc * conc * conc - (1.0 + STABILIZER) * conc)

    half = size // 2
    mob_x = pair_sum(pair_rows(level0.part(mob0, size + 4)), 1, 2) * 0.125
    rows_buf[: half + 2, :24] = mob_x
    rows_buf[: half + 2, 24:32] = mob_x[:, 16:24]
    mob1 = (
        rows_buf[: half + 2, pl.ds(0, 16, stride=2)] + rows_buf[: half + 2, pl.ds(1, 16, stride=2)]
    )
    mob1_sum = near_sum(mob1, 1, 2)[:, :8]
    mob1 = mob1[1:-1, :8]
    even1 = iota((half, 8, 128), 2) % 2 == 0
    whole1[1] = jnp.where(even1, mob1, mob1_sum)

    conc, chem = level0.sweep(conc, chem, right_side0)
    conc, chem = level0.sweep(conc, chem, right_side0)
    fields0 = (conc, chem)
    first, second = level0.residual(level0.part(conc, size + 2), level0.part(chem, size + 2), right_side0)

    def coarse_right(values):
        rows_buf[:half, :16] = pair_sum(pair_rows(values[:, :16]), 1, 2) * 0.125
        return rows_buf[:half, pl.ds(0, 8, stride=2)] + rows_buf[:half, pl.ds(1, 8, stride=2)]

    right_c = coarse_right(first)
    right_u = coarse_right(second)
    whole1[0] = jnp.where(even1, right_c, right_u)
    edge1[0] = split_halves(whole1[0], whole1[1], False, False)
    edge1[1] = split_halves(whole1[0], whole1[1], True, True)

    waits = []
    for side, dx in ((0, -1), (1, 1)):
        rows = pl.ds(0, HALO) if dx < 0 else pl.ds(half - HALO, HALO)
        waits.append(send(whole1.at[:, rows], from_x1.at[side], dx, 0))
    for place, (dx, dy) in enumerate(CORNERS):
        rows = pl.ds(0, HALO - 1) if dx < 0 else pl.ds(half - HALO + 1, HALO - 1)
        waits.append(send(edge1.at[(dy + 1) // 2, rows], from_d1.at[place], dx, dy))
    for side, dy in ((0, -1), (1, 1)):
        waits.append(send(edge1.at[side], from_y1.at[side], 0, dy))
    for copy in waits:
        copy.wait_recv()

    right1 = halo_rows(from_y1[0], (from_d1[0], from_d1[2]))
    left1 = halo_rows(from_y1[1], (from_d1[1], from_d1[3]))
    rhs_halo, mob_halo = joined(right1, left1)
    rhs1 = jnp.concatenate([from_x1[1, 0], whole1[0], from_x1[0, 0]], 0)
    mob1 = jnp.concatenate([from_x1[1, 1], whole1[1], from_x1[0, 1]], 0)
    rhs1 = jnp.concatenate([rhs1, rhs_halo], 1)
    mob1 = jnp.concatenate([mob1, mob_halo], 1)

    def spread(values, step, axis):
        low = (iota(values.shape, axis) // step) % 2 == 0
        return (
            jnp.where(low, values, turn(values, step, axis)),
            jnp.where(low, turn(values, -step, axis), values),
        )

    rhs1 = spread(rhs1, 1, 2)
    mob1, mob1_sum = spread(mob1, 1, 2)
    level1 = Level(0.25, mob1, mob1_sum, 1, 2)
    conc, chem = level1.step(*rhs1)
    conc, chem = level1.sweep(conc, chem, rhs1)
    fields1 = (conc, chem)
    first, second = level1.residual(level1.part(conc, half + 2), level1.part(chem, half + 2), rhs1)

    def coarse(values, row_step, lane_step):
        return pair_sum(pair_sum(pair_rows(values), row_step, 1), lane_step, 2) * 0.125

    quarter = half // 2
    own = (
        coarse(first[:, :8], 1, 2),
        coarse(second[:, :8], 1, 2),
        coarse(level1.part(mob1, half)[:, :8], 1, 2),
    )

    def by_lane(values):
        lane = iota((8, 128), 1) % 4
        return jnp.where(
            lane < 2,
            jnp.where(lane == 0, values[0], values[1]),
            jnp.where(lane == 2, values[2], values[3]),
        )

    pack2[0] = jnp.where(iota((8, 128), 0) % 2 == 0, by_lane(own[0]), by_lane(own[1]))
    pack2[1] = by_lane(own[2])
    waits = []
    for dx, dy in peers:
        slot = grid2.at[(nx - dx) % nx, (ny - dy) % ny]
        waits.append(send(pack2, slot, dx, dy))
    grid2[0, 0] = pack2[...]
    for copy in waits:
        copy.wait_recv()

    gathered = grid2[...]
    rhs2 = gathered[:, :, 0].reshape(nx, ny * 8, 128)
    mob2 = gathered[:, :, 1].reshape(nx, ny * 8, 128)

    def by_row(values):
        zero, one = spread(values, 1, 2)
        zero, two = spread(zero, 2, 2)
        one, three = spread(one, 2, 2)
        together = jnp.stack([zero, one, two, three], 1)
        return together.reshape((nx * quarter,) + values.shape[1:])

    rhs2 = tuple(by_row(v) for v in spread(rhs2, 1, 1))
    mob2 = by_row(mob2)
    level2 = Level(0.0625, mob2, near_sum(mob2, 2, 4, True), 2, 4, True)
    mob3 = coarse(mob2, 2, 4)
    level3 = Level(0.015625, mob3, near_sum(mob3, 4, 8, True), 4, 8, True)

    conc, chem = level2.step(*rhs2)
    conc, chem = level2.sweep(conc, chem, rhs2)
    rhs3 = tuple(coarse(v, 2, 4) for v in level2.residual(conc, chem, rhs2))
    low_conc, low_chem = level3.step(*rhs3)
    for _ in range(COARSE - 1):
        low_conc, low_chem = level3.sweep(low_conc, low_chem, rhs3)
    conc, chem = conc + twice(low_conc), chem + twice(low_chem)
    for _ in range(SWEEPS):
        conc, chem = level2.sweep(conc, chem, rhs2)

    def around1(values):
        values = jnp.concatenate([values[-2:], values[: quarter + 2]], 0)
        low = iota((quarter + 4, 8, 128), 1) < 4
        beside = jnp.where(low, values[:, 8:16], values[:, -8:])
        return twice(jnp.concatenate([values[:, :8], beside], 1))[1:-1]

    conc, chem = fields1[0] + around1(conc), fields1[1] + around1(chem)
    for _ in range(SWEEPS):
        conc, chem = level1.sweep(conc, chem, rhs1)

    def around0(values):
        count = values.shape[0]
        rows_buf[:count, pl.ds(0, 16, stride=2)] = values
        rows_buf[:count, pl.ds(1, 16, stride=2)] = values
        doubled = rows_buf[:count]
        low = iota((count, 8, 128), 1) < 4
        beside = jnp.where(low, doubled[:, 16:24], doubled[:, 24:32])
        return twice(jnp.concatenate([doubled[:, :16], beside], 1))

    conc, chem = fields0[0] + around0(conc), fields0[1] + around0(chem)
    for _ in range(SWEEPS):
        conc, chem = level0.sweep(conc, chem, right_side0)
    conc_out[...] = conc[:, :16]
    chem_out[...] = chem[:, :16]
    for copy in started:
        copy.wait_send()


def gathered_cycle(nx, ny, conc_old, chem_old):
    size = conc_old.shape[0]
    half = size // 2
    copies = 18 + nx * ny - 1
    scratch = [
        (2, size, 8, 128),
        (2, 2, HALO, 16, 128),
        (2, size, 8, 128),
        (4, HALO - 1, 8, 128),
        (2, half, 8, 128),
        (2, half, 8, 128),
        (2, 2, HALO, 8, 128),
        (2, half, 8, 128),
        (4, HALO - 1, 8, 128),
        (2, 8, 128),
        (nx, ny, 2, 8, 128),
        (half + 2, 32, 128),
    ]
    shape = jax.ShapeDtypeStruct(conc_old.shape, jnp.float32)
    space = pl.BlockSpec(memory_space=pltpu.VMEM)
    return pl.pallas_call(
        functools.partial(cycle_kernel, nx, ny),
        out_shape=(shape, shape),
        in_specs=[space, space],
        out_specs=(space, space),
        scratch_shapes=[pltpu.VMEM(dims, jnp.float32) for dims in scratch]
        + [pltpu.SemaphoreType.DMA((copies,)), pltpu.SemaphoreType.DMA((copies,))],
        compiler_params=pltpu.CompilerParams(
            collective_id=0, has_side_effects=True, vmem_limit_bytes=32 * 1024 * 1024
        ),
    )(conc_old, chem_old)


def body(conc_old, chem_old):
    nx, ny = lax.axis_size("gx"), lax.axis_size("gy")
    if conc_old.shape == (16, 16, 128) and min(nx, ny) >= 3 and nx * ny <= 16:
        return gathered_cycle(nx, ny, conc_old, chem_old)
    result = plain_solve(jnp.stack([conc_old, chem_old]))
    return (result[0], result[1])


def solution(mesh):
    in_specs = (P(("img", "gx"), "gy", None), P(("img", "gx"), "gy", None))
    out_specs = (P(("img", "gx"), "gy", None), P(("img", "gx"), "gy", None))
    return jax.shard_map(body, mesh=mesh, in_specs=in_specs, out_specs=out_specs, check_vma=False)
```

```python
import functools

import jax
import jax.numpy as jnp
from jax import lax
from jax.experimental import pallas as pl
from jax.experimental.pallas import tpu as pltpu
from jax.sharding import PartitionSpec as P

LEVELS = 4
SWEEPS = 2
COARSE = 6


TIME_STEP = 32.0
GRADIENT_ENERGY = 0.5
STABILIZER = 2.0
DAMPING = 0.7


def extended(cells, sides, width):
    for axis, dim in sides:
        count = lax.axis_size(axis)
        head = lax.slice_in_dim(cells, 0, width, axis=dim)
        tail = lax.slice_in_dim(cells, cells.shape[dim] - width, cells.shape[dim], axis=dim)
        cells = jnp.concatenate(
            [
                lax.ppermute(tail, axis, [(i, (i + 1) % count) for i in range(count)]),
                cells,
                lax.ppermute(head, axis, [((i + 1) % count, i) for i in range(count)]),
            ],
            axis=dim,
        )
    return cells


def mobility_of(concentration):
    return 0.1 + jnp.square(1.0 - concentration * concentration)


def right_of(concentration):
    return jnp.stack(
        [
            concentration,
            concentration * concentration * concentration - (1.0 + STABILIZER) * concentration,
        ]
    )


def face_weights(mob_padded, level_scale):
    middle = mob_padded[1:-1, 1:-1, :]
    half_scale = 0.5 * level_scale
    weights = (
        half_scale * (middle + mob_padded[2:, 1:-1, :]),
        half_scale * (middle + mob_padded[:-2, 1:-1, :]),
        half_scale * (middle + mob_padded[1:-1, 2:, :]),
        half_scale * (middle + mob_padded[1:-1, :-2, :]),
        half_scale * (middle + jnp.roll(middle, -1, axis=2)),
        half_scale * (middle + jnp.roll(middle, 1, axis=2)),
    )
    total_weight = weights[0] + weights[1] + weights[2] + weights[3] + weights[4] + weights[5]
    return (weights, total_weight)


def neighbour_list(padded, middle):
    return (
        padded[2:, 1:-1, :],
        padded[:-2, 1:-1, :],
        padded[1:-1, 2:, :],
        padded[1:-1, :-2, :],
        jnp.roll(middle, -1, axis=2),
        jnp.roll(middle, 1, axis=2),
    )


def apply_operator(padded, weights, level_scale):
    middle = padded[:, 1:-1, 1:-1, :]
    conc_near = neighbour_list(padded[0], middle[0])
    chem_near = neighbour_list(padded[1], middle[1])
    flux = weights[0] * (chem_near[0] - middle[1])
    for position in range(1, 6):
        flux = flux + weights[position] * (chem_near[position] - middle[1])
    laplace = (
        conc_near[0]
        + conc_near[1]
        + conc_near[2]
        + conc_near[3]
        + conc_near[4]
        + conc_near[5]
        - 6.0 * middle[0]
    )
    first_eq = middle[0] - TIME_STEP * flux
    second_eq = middle[1] - STABILIZER * middle[0] + GRADIENT_ENERGY * level_scale * laplace
    return jnp.stack([first_eq, second_eq])


def update(residual, total_weight, level_scale):
    diagonal = STABILIZER + 6.0 * GRADIENT_ENERGY * level_scale
    coupling = TIME_STEP * total_weight
    determinant = 1.0 + coupling * diagonal
    conc_step = (residual[0] - coupling * residual[1]) / determinant
    chem_step = (residual[1] + diagonal * residual[0]) / determinant
    return DAMPING * jnp.stack([conc_step, chem_step])


def sweep_once(padded, right_side, mob_padded, level_scale):
    weights, total_weight = face_weights(mob_padded, level_scale)
    residual = right_side - apply_operator(padded, weights, level_scale)
    return padded[:, 1:-1, 1:-1, :] + update(residual, total_weight, level_scale)


def defect(padded, right_side, mob_padded, level_scale):
    weights = face_weights(mob_padded, level_scale)[0]
    return right_side - apply_operator(padded, weights, level_scale)


def coarsen(values):
    dims_now = values.shape
    grouped = values.reshape(
        dims_now[:-3] + (dims_now[-3] // 2, 2, dims_now[-2] // 2, 2, dims_now[-1] // 2, 2)
    )
    return jnp.sum(grouped, axis=(-5, -3, -1)) * 0.125


def refine(values):
    for axis_pos in (-3, -2, -1):
        values = jnp.repeat(values, 2, axis=axis_pos)
    return values


def trim_rim(values, width):
    return values[..., width:-width, width:-width, :]


def field_rim(fields):
    return extended(fields, (("gx", 1), ("gy", 2)), 1)


def coarsest_solve(right_side, mobility, level_scale):
    mob_padded = extended(mobility, (("gx", 0), ("gy", 1)), 1)
    fields = update(right_side, face_weights(mob_padded, level_scale)[1], level_scale)
    for sweep_index in range(COARSE - 1):
        padded = extended(fields, (("gx", 1), ("gy", 2)), 1)
        fields = sweep_once(padded, right_side, mob_padded, level_scale)
    return fields


def plain_solve(start_fields):
    outer_fields = field_rim(start_fields)
    mob_outer = mobility_of(outer_fields[0])
    mobility = trim_rim(mob_outer, 1)
    level_data = []
    for level_index in range(LEVELS - 1):
        if level_index == 0:
            mob_padded = mob_outer
        else:
            mob_padded = extended(mobility, (("gx", 0), ("gy", 1)), 1)
        level_data.append((mob_padded, 0.25**level_index))
        mobility = coarsen(mobility)
    coarsest_scale = 0.25 ** (LEVELS - 1)

    def cycle_level(level_index, right_side):
        if level_index == LEVELS - 1:
            return coarsest_solve(right_side, mobility, coarsest_scale)
        mob_padded, level_scale = level_data[level_index]
        if level_index == 0:
            fields = sweep_once(outer_fields, right_side, mob_padded, level_scale)
        else:
            fields = update(right_side, face_weights(mob_padded, level_scale)[1], level_scale)
        fields = sweep_once(field_rim(fields), right_side, mob_padded, level_scale)
        residual = defect(field_rim(fields), right_side, mob_padded, level_scale)
        fields = fields + refine(cycle_level(level_index + 1, coarsen(residual)))
        for sweep_index in range(SWEEPS):
            fields = sweep_once(field_rim(fields), right_side, mob_padded, level_scale)
        return fields

    return cycle_level(0, right_of(start_fields[0]))


MESH = pl.DeviceIdType.MESH
HALO = 4
SIDES = (("lo", -1), ("hi", 1))
CORNERS = ((-1, -1), (-1, 1), (1, -1), (1, 1))


def iota(shape, dim):
    return lax.broadcasted_iota(jnp.int32, shape, dim)


def turn(values, shift, axis):
    size = values.shape[axis]
    return pltpu.roll(values, shift % size, axis)


def near_sum(values, row_step, lane_step, wrap=False):
    if wrap:
        middle = values
        total = jnp.concatenate([values[1:], values[:1]], 0) + jnp.concatenate(
            [values[-1:], values[:-1]], 0
        )
    else:
        middle = values[1:-1]
        total = values[2:] + values[:-2]
    total = total + (turn(middle, row_step, 1) + turn(middle, -row_step, 1))
    return total + (turn(middle, lane_step, 2) + turn(middle, -lane_step, 2))


def pair_sum(values, step, axis):
    low = (iota(values.shape, axis) // step) % 2 == 0
    return values + jnp.where(low, turn(values, -step, axis), turn(values, step, axis))


def pair_rows(values):
    grouped = values.reshape((values.shape[0] // 2, 2) + values.shape[1:])
    return grouped[:, 0] + grouped[:, 1]


def twice(values):
    return jnp.concatenate([values[i // 2 : i // 2 + 1] for i in range(2 * values.shape[0])], 0)


class Level:
    def __init__(self, scale, mob, mob_sum, row_step, lane_step, wrap=False):
        self.scale, self.mob = scale, mob
        self.row_step, self.lane_step, self.wrap = row_step, lane_step, wrap
        self.half = 0.5 * TIME_STEP * scale
        self.diagonal = STABILIZER + 6.0 * GRADIENT_ENERGY * scale
        self.coupling = self.half * (6.0 * mob + mob_sum)
        self.damp = DAMPING / (1.0 + self.coupling * self.diagonal)

    def part(self, values, size):
        off = (values.shape[0] - size) // 2
        return values[off : off + size]

    def residual(self, conc, chem, right):
        size = conc.shape[0] if self.wrap else conc.shape[0] - 2
        sums = functools.partial(
            near_sum, row_step=self.row_step, lane_step=self.lane_step, wrap=self.wrap
        )
        carried = self.part(self.mob, conc.shape[0]) * chem
        mob = self.part(self.mob, size)
        c, u = self.part(conc, size), self.part(chem, size)
        first = (
            self.part(right[0], size)
            - c
            + self.half * (mob * sums(chem) + sums(carried))
            - self.part(self.coupling, size) * u
        )
        near = sums(conc) - 6.0 * c
        second = (
            self.part(right[1], size)
            - u
            + STABILIZER * c
            - (GRADIENT_ENERGY * self.scale) * near
        )
        return first, second

    def step(self, first, second):
        size = first.shape[0]
        damp = self.part(self.damp, size)
        coupling = self.part(self.coupling, size)
        return damp * (first - coupling * second), damp * (second + self.diagonal * first)

    def sweep(self, conc, chem, right):
        first, second = self.residual(conc, chem, right)
        size = first.shape[0]
        dc, du = self.step(first, second)
        return self.part(conc, size) + dc, self.part(chem, size) + du


def split_halves(first, second, first_high, second_high):
    low = iota(first.shape, 1) < 4
    first = turn(first, 4, 1) if first_high else first
    second = second if second_high else turn(second, 4, 1)
    return jnp.where(low, first, second)


def cycle_kernel(nx, ny, conc_ref, chem_ref, conc_out, chem_out, *scratch):
    (
        own_conc,
        own_chem,
        edge0,
        from_x0,
        from_y0,
        from_d0,
        whole1,
        edge1,
        from_x1,
        from_y1,
        from_d1,
        pack2,
        grid2,
        rows_buf,
        load_sem,
        send_sem,
        recv_sem,
    ) = scratch
    img, gx, gy = lax.axis_index("img"), lax.axis_index("gx"), lax.axis_index("gy")
    loads = [
        pltpu.make_async_copy(conc_ref, own_conc, load_sem.at[0]),
        pltpu.make_async_copy(chem_ref, own_chem, load_sem.at[1]),
    ]
    for load in loads:
        load.start()

    def at(dx, dy):
        return (img, lax.rem(gx + dx + nx, nx), lax.rem(gy + dy + ny, ny))

    peers = [(dx, dy) for dx in range(nx) for dy in range(ny) if (dx, dy) != (0, 0)]
    barrier = pltpu.get_barrier_semaphore()
    for dx, dy in peers:
        pl.semaphore_signal(barrier, inc=1, device_id=at(dx, dy), device_id_type=MESH)

    used = [0]
    started = []

    def send(src, dst, dx, dy):
        index = used[0]
        used[0] += 1
        copy = pltpu.make_async_remote_copy(
            src_ref=src,
            dst_ref=dst,
            send_sem=send_sem.at[index],
            recv_sem=recv_sem.at[index],
            device_id=at(dx, dy),
            device_id_type=MESH,
        )
        copy.start()
        started.append(copy)
        return copy

    def arrive(copies):
        for copy in copies:
            copy.wait_recv()

    for load in loads:
        load.wait()
    size = own_conc.shape[0]
    half = size // 2
    quarter = half // 2
    conc, chem = own_conc[...], own_chem[...]
    edge0[0] = split_halves(conc[:, :8], chem[:, :8], False, False)
    edge0[1] = split_halves(conc[:, -8:], chem[:, -8:], True, True)
    pl.semaphore_wait(barrier, len(peers))

    waits = []
    for side, dx in ((0, -1), (1, 1)):
        rows = pl.ds(0, HALO) if dx < 0 else pl.ds(size - HALO, HALO)
        waits.append(send(own_conc.at[rows], from_x0.at[side, 0], dx, 0))
        waits.append(send(own_chem.at[rows], from_x0.at[side, 1], dx, 0))
    for place, (dx, dy) in enumerate(CORNERS):
        rows = pl.ds(0, HALO - 1) if dx < 0 else pl.ds(size - HALO + 1, HALO - 1)
        waits.append(send(edge0.at[(dy + 1) // 2, rows], from_d0.at[place], dx, dy))
    for side, dy in ((0, -1), (1, 1)):
        waits.append(send(edge0.at[side], from_y0.at[side], 0, dy))
    arrive(waits)

    def halo_rows(center, lower, upper):
        return jnp.concatenate([lower[:1], lower, center, upper, upper[-1:]], 0)

    def joined(right, left):
        low = iota(right.shape, 1) < 4
        return jnp.where(low, right, turn(left, 4, 1)), jnp.where(low, turn(right, 4, 1), left)

    right0 = halo_rows(from_y0[0], from_d0[2], from_d0[0])
    left0 = halo_rows(from_y0[1], from_d0[3], from_d0[1])
    conc_halo, chem_halo = joined(right0, left0)
    conc = jnp.concatenate([from_x0[1, 0], conc, from_x0[0, 0]], 0)
    chem = jnp.concatenate([from_x0[1, 1], chem, from_x0[0, 1]], 0)
    conc = jnp.concatenate([conc, conc_halo], 1)
    chem = jnp.concatenate([chem, chem_halo], 1)

    def row_pairs(values):
        count, rows = values.shape[:2]
        rows_buf[:count, :rows] = values
        return (
            rows_buf[:count, pl.ds(0, rows // 2, stride=2)]
            + rows_buf[:count, pl.ds(1, rows // 2, stride=2)]
        )

    def rows_twice(values):
        count, rows = values.shape[:2]
        rows_buf[:count, pl.ds(0, rows, stride=2)] = values
        rows_buf[:count, pl.ds(1, rows, stride=2)] = values
        return rows_buf[:count, : 2 * rows]

    def coarse(values, lane_step):
        return row_pairs(pair_sum(pair_rows(values), lane_step, 2) * 0.125)

    def spread(values, step, axis):
        low = (iota(values.shape, axis) // step) % 2 == 0
        return (
            jnp.where(low, values, turn(values, step, axis)),
            jnp.where(low, turn(values, -step, axis), values),
        )

    def by_lane(values):
        lane = iota((8, 128), 1) % 4
        return jnp.where(
            lane < 2,
            jnp.where(lane == 0, values[0], values[1]),
            jnp.where(lane == 2, values[2], values[3]),
        )

    def twice_pair(values):
        return pair_sum(values, 1, 1)

    def gather(kind):
        copies = []
        for dx, dy in peers:
            rows = pl.ds(8 * ((ny - dy) % ny), 8)
            copies.append(send(pack2.at[kind], grid2.at[kind, (nx - dx) % nx, rows], dx, dy))
        grid2[kind, 0, :8] = pack2[kind]
        return copies

    def swap1(kind, inner):
        first, rest = [], []
        edge1[kind, 0] = split_halves(whole1[kind, :4], whole1[kind, 4:], False, False)
        edge1[kind, 1] = split_halves(whole1[kind, :4], whole1[kind, 4:], True, True)

        def move(copies, src, dst, start, count, dx, dy, shift=0):
            if count > 0:
                source = src.at[pl.ds(start + shift, count)]
                copies.append(send(source, dst.at[pl.ds(start, count)], dx, dy))

        for copies in (first, rest):
            near = copies is first
            for side, dx in ((0, -1), (1, 1)):
                count = inner if near else HALO - inner
                start = 0 if (dx < 0) == near else HALO - count
                shift = 0 if dx < 0 else half - HALO
                move(copies, whole1.at[kind], from_x1.at[kind, side], start, count, dx, 0, shift)
            for place, (dx, dy) in enumerate(CORNERS):
                count = inner - 1 if near else HALO - inner
                if dx < 0:
                    start = 0 if near else inner - 1
                else:
                    start = HALO - inner + 1 if near else 1
                source = edge1.at[kind, (dy + 1) // 2]
                move(copies, source, from_d1.at[kind, place], start, count, dx, dy)
            if near:
                for side, dy in ((0, -1), (1, 1)):
                    copies.append(send(edge1.at[kind, side], from_y1.at[kind, side], 0, dy))
        return first, rest

    def padded1(kind, width):
        below, above = pl.ds(HALO - width + 1, width - 1), pl.ds(0, width - 1)
        lower = joined(from_d1[kind, 2, below], from_d1[kind, 3, below])[1]
        upper = joined(from_d1[kind, 0, above], from_d1[kind, 1, above])[0]
        center = jnp.concatenate(joined(from_y1[kind, 0], from_y1[kind, 1]), 0)
        inside = [from_x1[kind, 1, HALO - width :], whole1[kind], from_x1[kind, 0, :width]]
        return jnp.concatenate(
            [jnp.concatenate(inside, 0), halo_rows(center, lower, upper)], 1
        )

    mob0 = mobility_of(conc)
    mob_x = pair_sum(pair_rows(mob0[2:-2]), 1, 2) * 0.125
    mob1 = row_pairs(jnp.concatenate([mob_x, mob_x[:, 16:24]], 1))
    mob1_sum = near_sum(mob1, 1, 2)[:, :8]
    mob1 = mob1[1:-1, :8]
    even1 = iota((half, 8, 128), 2) % 2 == 0
    whole1[1] = jnp.where(even1, mob1, mob1_sum)
    mob1_waits, _ = swap1(1, HALO)
    pack2[1] = by_lane(twice_pair(pair_sum(pair_rows(mob1), 2, 2) * 0.125))
    mob2_waits = gather(1)

    level0 = Level(1.0, mob0[1:-1], near_sum(mob0, 1, 1), 1, 1)
    level0.mob = mob0
    right_side0 = (conc, conc * conc * conc - (1.0 + STABILIZER) * conc)
    conc, chem = level0.sweep(conc, chem, right_side0)
    conc, chem = level0.sweep(conc, chem, right_side0)
    fields0 = (conc, chem)
    first, second = level0.residual(
        level0.part(conc, size + 2), level0.part(chem, size + 2), right_side0
    )
    whole1[0] = jnp.where(even1, coarse(first[:, :16], 1), coarse(second[:, :16], 1))
    near_waits, far_waits = swap1(0, 2)

    arrive(mob1_waits)
    mob1, mob1_sum = spread(padded1(1, HALO), 1, 2)
    level1 = Level(0.25, mob1, mob1_sum, 1, 2)
    arrive(near_waits)
    rhs1 = spread(padded1(0, 2), 1, 2)
    conc, chem = level1.step(*rhs1)
    conc, chem = level1.sweep(conc, chem, rhs1)
    own = [
        twice_pair(pair_sum(pair_rows(values[:, :8]), 2, 2) * 0.125)
        for values in level1.residual(conc, chem, rhs1)
    ]
    pack2[0] = jnp.where(iota((8, 128), 0) % 2 == 0, by_lane(own[0]), by_lane(own[1]))
    rhs2_waits = gather(0)

    arrive(far_waits)
    rhs1 = spread(padded1(0, HALO), 1, 2)
    conc, chem = level1.step(*rhs1)
    fields1 = level1.sweep(conc, chem, rhs1)

    def by_row(values):
        zero, one = spread(values, 1, 2)
        zero, two = spread(zero, 2, 2)
        one, three = spread(one, 2, 2)
        together = jnp.stack([zero, one, two, three], 1)
        return together.reshape((nx * quarter,) + values.shape[1:])

    arrive(mob2_waits)
    mob2 = by_row(grid2[1, :, pl.ds(0, 4 * ny, stride=2)])
    level2 = Level(0.0625, mob2, near_sum(mob2, 1, 4, True), 1, 4, True)
    mob3 = coarse(mob2, 4)
    level3 = Level(0.015625, mob3, near_sum(mob3, 1, 8, True), 1, 8, True)

    arrive(rhs2_waits)
    rhs2 = [by_row(grid2[0, :, pl.ds(start, 4 * ny, stride=2)]) for start in (0, 1)]
    conc, chem = level2.step(*rhs2)
    conc, chem = level2.sweep(conc, chem, rhs2)
    rhs3 = [coarse(v, 4) for v in level2.residual(conc, chem, rhs2)]
    low_conc, low_chem = level3.step(*rhs3)
    for _ in range(COARSE - 1):
        low_conc, low_chem = level3.sweep(low_conc, low_chem, rhs3)
    conc = conc + twice(rows_twice(low_conc))
    chem = chem + twice(rows_twice(low_chem))
    for _ in range(SWEEPS):
        conc, chem = level2.sweep(conc, chem, rhs2)

    def around1(values):
        values = jnp.concatenate([values[-2:], values[: quarter + 2]], 0)
        values = rows_twice(values)
        low = iota((quarter + 4, 8, 128), 1) < 4
        beside = jnp.where(low, values[:, 8:16], values[:, -8:])
        return twice(jnp.concatenate([values[:, :8], beside], 1))[1:-1]

    conc, chem = fields1[0] + around1(conc), fields1[1] + around1(chem)
    for _ in range(SWEEPS):
        conc, chem = level1.sweep(conc, chem, rhs1)

    def around0(values):
        doubled = rows_twice(values)
        low = iota((values.shape[0], 8, 128), 1) < 4
        beside = jnp.where(low, doubled[:, 16:24], doubled[:, 24:32])
        return twice(jnp.concatenate([doubled[:, :16], beside], 1))

    conc, chem = fields0[0] + around0(conc), fields0[1] + around0(chem)
    for _ in range(SWEEPS):
        conc, chem = level0.sweep(conc, chem, right_side0)
    conc_out[...] = conc[:, :16]
    chem_out[...] = chem[:, :16]
    for copy in started:
        copy.wait_send()


def gathered_cycle(nx, ny, conc_old, chem_old):
    size = conc_old.shape[0]
    half = size // 2
    copies = 10 + 8 + 14 + 2 * (nx * ny - 1)
    scratch = [
        conc_old.shape,
        conc_old.shape,
        (2, size, 8, 128),
        (2, 2, HALO, 16, 128),
        (2, size, 8, 128),
        (4, HALO - 1, 8, 128),
        (2, half, 8, 128),
        (2, 2, half // 2, 8, 128),
        (2, 2, HALO, 8, 128),
        (2, 2, half // 2, 8, 128),
        (2, 4, HALO, 8, 128),
        (2, 8, 128),
        (2, nx, ny * 8, 128),
        (2 * nx + half, 8 * ny, 128),
    ]
    shape = jax.ShapeDtypeStruct(conc_old.shape, jnp.float32)
    space = pl.BlockSpec(memory_space=pltpu.VMEM)
    away = pl.BlockSpec(memory_space=pl.ANY)
    return pl.pallas_call(
        functools.partial(cycle_kernel, nx, ny),
        out_shape=(shape, shape),
        in_specs=[away, away],
        out_specs=(space, space),
        scratch_shapes=[pltpu.VMEM(dims, jnp.float32) for dims in scratch]
        + [pltpu.SemaphoreType.DMA((count,)) for count in (2, copies, copies)],
        compiler_params=pltpu.CompilerParams(
            collective_id=0, has_side_effects=True, vmem_limit_bytes=32 * 1024 * 1024
        ),
    )(conc_old, chem_old)


def body(conc_old, chem_old):
    nx, ny = lax.axis_size("gx"), lax.axis_size("gy")
    if conc_old.shape == (16, 16, 128) and nx >= 3 and ny == 4 and nx * ny <= 16:
        return gathered_cycle(nx, ny, conc_old, chem_old)
    result = plain_solve(jnp.stack([conc_old, chem_old]))
    return (result[0], result[1])


def solution(mesh):
    in_specs = (P(("img", "gx"), "gy", None), P(("img", "gx"), "gy", None))
    out_specs = (P(("img", "gx"), "gy", None), P(("img", "gx"), "gy", None))
    return jax.shard_map(body, mesh=mesh, in_specs=in_specs, out_specs=out_specs, check_vma=False)
```

```python
import functools

import jax
import jax.numpy as jnp
from jax import lax
from jax.experimental import pallas as pl
from jax.experimental.pallas import tpu as pltpu
from jax.sharding import PartitionSpec as P

LEVELS = 4
SWEEPS = 2
COARSE = 6


TIME_STEP = 32.0
GRADIENT_ENERGY = 0.5
STABILIZER = 2.0
DAMPING = 0.7


def extended(cells, sides, width):
    for axis, dim in sides:
        count = lax.axis_size(axis)
        head = lax.slice_in_dim(cells, 0, width, axis=dim)
        tail = lax.slice_in_dim(cells, cells.shape[dim] - width, cells.shape[dim], axis=dim)
        cells = jnp.concatenate(
            [
                lax.ppermute(tail, axis, [(i, (i + 1) % count) for i in range(count)]),
                cells,
                lax.ppermute(head, axis, [((i + 1) % count, i) for i in range(count)]),
            ],
            axis=dim,
        )
    return cells


def mobility_of(concentration):
    return 0.1 + jnp.square(1.0 - concentration * concentration)


def right_of(concentration):
    return jnp.stack(
        [
            concentration,
            concentration * concentration * concentration - (1.0 + STABILIZER) * concentration,
        ]
    )


def face_weights(mob_padded, level_scale):
    middle = mob_padded[1:-1, 1:-1, :]
    half_scale = 0.5 * level_scale
    weights = (
        half_scale * (middle + mob_padded[2:, 1:-1, :]),
        half_scale * (middle + mob_padded[:-2, 1:-1, :]),
        half_scale * (middle + mob_padded[1:-1, 2:, :]),
        half_scale * (middle + mob_padded[1:-1, :-2, :]),
        half_scale * (middle + jnp.roll(middle, -1, axis=2)),
        half_scale * (middle + jnp.roll(middle, 1, axis=2)),
    )
    total_weight = weights[0] + weights[1] + weights[2] + weights[3] + weights[4] + weights[5]
    return (weights, total_weight)


def neighbour_list(padded, middle):
    return (
        padded[2:, 1:-1, :],
        padded[:-2, 1:-1, :],
        padded[1:-1, 2:, :],
        padded[1:-1, :-2, :],
        jnp.roll(middle, -1, axis=2),
        jnp.roll(middle, 1, axis=2),
    )


def apply_operator(padded, weights, level_scale):
    middle = padded[:, 1:-1, 1:-1, :]
    conc_near = neighbour_list(padded[0], middle[0])
    chem_near = neighbour_list(padded[1], middle[1])
    flux = weights[0] * (chem_near[0] - middle[1])
    for position in range(1, 6):
        flux = flux + weights[position] * (chem_near[position] - middle[1])
    laplace = (
        conc_near[0]
        + conc_near[1]
        + conc_near[2]
        + conc_near[3]
        + conc_near[4]
        + conc_near[5]
        - 6.0 * middle[0]
    )
    first_eq = middle[0] - TIME_STEP * flux
    second_eq = middle[1] - STABILIZER * middle[0] + GRADIENT_ENERGY * level_scale * laplace
    return jnp.stack([first_eq, second_eq])


def update(residual, total_weight, level_scale):
    diagonal = STABILIZER + 6.0 * GRADIENT_ENERGY * level_scale
    coupling = TIME_STEP * total_weight
    determinant = 1.0 + coupling * diagonal
    conc_step = (residual[0] - coupling * residual[1]) / determinant
    chem_step = (residual[1] + diagonal * residual[0]) / determinant
    return DAMPING * jnp.stack([conc_step, chem_step])


def sweep_once(padded, right_side, mob_padded, level_scale):
    weights, total_weight = face_weights(mob_padded, level_scale)
    residual = right_side - apply_operator(padded, weights, level_scale)
    return padded[:, 1:-1, 1:-1, :] + update(residual, total_weight, level_scale)


def defect(padded, right_side, mob_padded, level_scale):
    weights = face_weights(mob_padded, level_scale)[0]
    return right_side - apply_operator(padded, weights, level_scale)


def coarsen(values):
    dims_now = values.shape
    grouped = values.reshape(
        dims_now[:-3] + (dims_now[-3] // 2, 2, dims_now[-2] // 2, 2, dims_now[-1] // 2, 2)
    )
    return jnp.sum(grouped, axis=(-5, -3, -1)) * 0.125


def refine(values):
    for axis_pos in (-3, -2, -1):
        values = jnp.repeat(values, 2, axis=axis_pos)
    return values


def trim_rim(values, width):
    return values[..., width:-width, width:-width, :]


def field_rim(fields):
    return extended(fields, (("gx", 1), ("gy", 2)), 1)


def coarsest_solve(right_side, mobility, level_scale):
    mob_padded = extended(mobility, (("gx", 0), ("gy", 1)), 1)
    fields = update(right_side, face_weights(mob_padded, level_scale)[1], level_scale)
    for sweep_index in range(COARSE - 1):
        padded = extended(fields, (("gx", 1), ("gy", 2)), 1)
        fields = sweep_once(padded, right_side, mob_padded, level_scale)
    return fields


def plain_solve(start_fields):
    outer_fields = field_rim(start_fields)
    mob_outer = mobility_of(outer_fields[0])
    mobility = trim_rim(mob_outer, 1)
    level_data = []
    for level_index in range(LEVELS - 1):
        if level_index == 0:
            mob_padded = mob_outer
        else:
            mob_padded = extended(mobility, (("gx", 0), ("gy", 1)), 1)
        level_data.append((mob_padded, 0.25**level_index))
        mobility = coarsen(mobility)
    coarsest_scale = 0.25 ** (LEVELS - 1)

    def cycle_level(level_index, right_side):
        if level_index == LEVELS - 1:
            return coarsest_solve(right_side, mobility, coarsest_scale)
        mob_padded, level_scale = level_data[level_index]
        if level_index == 0:
            fields = sweep_once(outer_fields, right_side, mob_padded, level_scale)
        else:
            fields = update(right_side, face_weights(mob_padded, level_scale)[1], level_scale)
        fields = sweep_once(field_rim(fields), right_side, mob_padded, level_scale)
        residual = defect(field_rim(fields), right_side, mob_padded, level_scale)
        fields = fields + refine(cycle_level(level_index + 1, coarsen(residual)))
        for sweep_index in range(SWEEPS):
            fields = sweep_once(field_rim(fields), right_side, mob_padded, level_scale)
        return fields

    return cycle_level(0, right_of(start_fields[0]))


MESH = pl.DeviceIdType.MESH
HALO = 4
SIDES = (("lo", -1), ("hi", 1))
CORNERS = ((-1, -1), (-1, 1), (1, -1), (1, 1))


def iota(shape, dim):
    return lax.broadcasted_iota(jnp.int32, shape, dim)


def turn(values, shift, axis):
    size = values.shape[axis]
    return pltpu.roll(values, shift % size, axis)


def near_sum(values, row_step, lane_step, wrap=False):
    if wrap:
        middle = values
        total = jnp.concatenate([values[1:], values[:1]], 0) + jnp.concatenate(
            [values[-1:], values[:-1]], 0
        )
    else:
        middle = values[1:-1]
        total = values[2:] + values[:-2]
    total = total + (turn(middle, row_step, 1) + turn(middle, -row_step, 1))
    return total + (turn(middle, lane_step, 2) + turn(middle, -lane_step, 2))


def pair_sum(values, step, axis):
    low = (iota(values.shape, axis) // step) % 2 == 0
    return values + jnp.where(low, turn(values, -step, axis), turn(values, step, axis))


def pair_rows(values):
    grouped = values.reshape((values.shape[0] // 2, 2) + values.shape[1:])
    return grouped[:, 0] + grouped[:, 1]


def twice(values):
    return jnp.concatenate([values[i // 2 : i // 2 + 1] for i in range(2 * values.shape[0])], 0)


class Strip:
    def __init__(self, start, cells):
        self.start, self.cells = start, cells

    def at(self, low, high):
        return self.cells[low - self.start : high - self.start]


def strips(*parts):
    return Strip(parts[0].start, jnp.concatenate([part.cells for part in parts], 0))


class Level:
    def __init__(self, scale, row_step, lane_step, wrap=False):
        self.scale = scale
        self.row_step, self.lane_step, self.wrap = row_step, lane_step, wrap
        self.half = 0.5 * TIME_STEP * scale
        self.diagonal = STABILIZER + 6.0 * GRADIENT_ENERGY * scale
        self.mob = self.coupling = self.damp = None

    def set(self, mob, coupling):
        self.mob = mob
        self.coupling = coupling
        self.damp = Strip(coupling.start, DAMPING / (1.0 + coupling.cells * self.diagonal))
        return self

    def sums(self, values):
        return near_sum(values, self.row_step, self.lane_step, self.wrap)

    def coupled(self, mob, mob_sum):
        return self.half * (6.0 * mob + mob_sum)

    def residual(self, conc, chem, right, low, high):
        rim = 0 if self.wrap else 1
        c, u, mob = conc.at(low, high), chem.at(low, high), self.mob.at(low, high)
        near_chem = chem.at(low - rim, high + rim)
        carried = self.mob.at(low - rim, high + rim) * near_chem
        first = (
            right[0].at(low, high)
            - c
            + self.half * (mob * self.sums(near_chem) + self.sums(carried))
            - self.coupling.at(low, high) * u
        )
        near = self.sums(conc.at(low - rim, high + rim)) - 6.0 * c
        second = (
            right[1].at(low, high)
            - u
            + STABILIZER * c
            - (GRADIENT_ENERGY * self.scale) * near
        )
        return first, second

    def step(self, first, second, low):
        high = low + first.shape[0]
        damp = self.damp.at(low, high)
        coupling = self.coupling.at(low, high)
        conc_step = damp * (first - coupling * second)
        return Strip(low, conc_step), Strip(low, damp * (second + self.diagonal * first))

    def sweep(self, conc, chem, right, low, high):
        dc, du = self.step(*self.residual(conc, chem, right, low, high), low)
        return Strip(low, conc.at(low, high) + dc.cells), Strip(low, chem.at(low, high) + du.cells)

    def sweeps(self, count, conc, chem, right):
        size = conc.cells.shape[0]

        def once(_, now):
            new = self.sweep(Strip(0, now[0]), Strip(0, now[1]), right, 0, size)
            return new[0].cells, new[1].cells

        now = lax.fori_loop(0, count, once, (conc.cells, chem.cells))
        return Strip(0, now[0]), Strip(0, now[1])


def split_halves(first, second, first_high, second_high):
    low = iota(first.shape, 1) < 4
    first = turn(first, 4, 1) if first_high else first
    second = second if second_high else turn(second, 4, 1)
    return jnp.where(low, first, second)


def cycle_kernel(nx, ny, conc_ref, chem_ref, conc_out, chem_out, *scratch):
    (
        own_conc,
        own_chem,
        edge0,
        from_x0,
        from_y0,
        from_d0,
        whole1,
        edge1,
        from_x1,
        from_y1,
        from_d1,
        pack2,
        grid2,
        rows_buf,
        load_sem,
        send_sem,
        recv_sem,
    ) = scratch
    img, gx, gy = lax.axis_index("img"), lax.axis_index("gx"), lax.axis_index("gy")
    loads = [
        pltpu.make_async_copy(conc_ref, own_conc, load_sem.at[0]),
        pltpu.make_async_copy(chem_ref, own_chem, load_sem.at[1]),
    ]
    for load in loads:
        load.start()

    def at(dx, dy):
        return (img, lax.rem(gx + dx + nx, nx), lax.rem(gy + dy + ny, ny))

    peers = [(dx, dy) for dx in range(nx) for dy in range(ny) if (dx, dy) != (0, 0)]
    barrier = pltpu.get_barrier_semaphore()
    for dx, dy in peers:
        pl.semaphore_signal(barrier, inc=1, device_id=at(dx, dy), device_id_type=MESH)

    used = [0]
    started = []

    def send(src, dst, dx, dy):
        index = used[0]
        used[0] += 1
        copy = pltpu.make_async_remote_copy(
            src_ref=src,
            dst_ref=dst,
            send_sem=send_sem.at[index],
            recv_sem=recv_sem.at[index],
            device_id=at(dx, dy),
            device_id_type=MESH,
        )
        copy.start()
        started.append(copy)
        return copy

    def arrive(copies):
        for copy in copies:
            copy.wait_recv()

    for load in loads:
        load.wait()
    size = own_conc.shape[0]
    half = size // 2
    quarter = half // 2
    conc, chem = own_conc[...], own_chem[...]
    edge0[0] = split_halves(conc[:, :8], chem[:, :8], False, False)
    edge0[1] = split_halves(conc[:, -8:], chem[:, -8:], True, True)
    pl.semaphore_wait(barrier, len(peers))

    outer, beside = [], []
    for side, dx in ((0, -1), (1, 1)):
        rows = pl.ds(0, HALO) if dx < 0 else pl.ds(size - HALO, HALO)
        outer.append(send(own_conc.at[rows], from_x0.at[side, 0], dx, 0))
        outer.append(send(own_chem.at[rows], from_x0.at[side, 1], dx, 0))
    for side, dy in ((0, -1), (1, 1)):
        beside.append(send(edge0.at[side], from_y0.at[side], 0, dy))
    for place, (dx, dy) in enumerate(CORNERS):
        rows = pl.ds(0, HALO - 1) if dx < 0 else pl.ds(size - HALO + 1, HALO - 1)
        outer.append(send(edge0.at[(dy + 1) // 2, rows], from_d0.at[place], dx, dy))

    def halo_rows(center, lower, upper):
        return jnp.concatenate([lower[:1], lower, center, upper, upper[-1:]], 0)

    def joined(right, left):
        low = iota(right.shape, 1) < 4
        return jnp.where(low, right, turn(left, 4, 1)), jnp.where(low, turn(right, 4, 1), left)

    def row_pairs(values):
        count, rows = values.shape[:2]
        rows_buf[:count, :rows] = values
        return (
            rows_buf[:count, pl.ds(0, rows // 2, stride=2)]
            + rows_buf[:count, pl.ds(1, rows // 2, stride=2)]
        )

    def rows_twice(values):
        count, rows = values.shape[:2]
        rows_buf[:count, pl.ds(0, rows, stride=2)] = values
        rows_buf[:count, pl.ds(1, rows, stride=2)] = values
        return rows_buf[:count, : 2 * rows]

    def coarse(values, lane_step):
        return row_pairs(pair_sum(pair_rows(values), lane_step, 2) * 0.125)

    def spread(values, step, axis):
        low = (iota(values.shape, axis) // step) % 2 == 0
        return (
            jnp.where(low, values, turn(values, step, axis)),
            jnp.where(low, turn(values, -step, axis), values),
        )

    def by_lane(values):
        lane = iota((8, 128), 1) % 4
        return jnp.where(
            lane < 2,
            jnp.where(lane == 0, values[0], values[1]),
            jnp.where(lane == 2, values[2], values[3]),
        )

    def twice_pair(values):
        return pair_sum(values, 1, 1)

    def gather(kind):
        copies = []
        for dx, dy in peers:
            rows = pl.ds(8 * ((ny - dy) % ny), 8)
            copies.append(send(pack2.at[kind], grid2.at[kind, (nx - dx) % nx, rows], dx, dy))
        grid2[kind, 0, :8] = pack2[kind]
        return copies

    def swap1(kind, inner):
        first, rest = [], []
        edge1[kind, 0] = split_halves(whole1[kind, :4], whole1[kind, 4:], False, False)
        edge1[kind, 1] = split_halves(whole1[kind, :4], whole1[kind, 4:], True, True)

        def move(copies, src, dst, start, count, dx, dy, shift=0):
            if count > 0:
                source = src.at[pl.ds(start + shift, count)]
                copies.append(send(source, dst.at[pl.ds(start, count)], dx, dy))

        for copies in (first, rest):
            near = copies is first
            for side, dx in ((0, -1), (1, 1)):
                count = inner if near else HALO - inner
                start = 0 if (dx < 0) == near else HALO - count
                shift = 0 if dx < 0 else half - HALO
                move(copies, whole1.at[kind], from_x1.at[kind, side], start, count, dx, 0, shift)
            for place, (dx, dy) in enumerate(CORNERS):
                count = inner - 1 if near else HALO - inner
                if dx < 0:
                    start = 0 if near else inner - 1
                else:
                    start = HALO - inner + 1 if near else 1
                source = edge1.at[kind, (dy + 1) // 2]
                move(copies, source, from_d1.at[kind, place], start, count, dx, dy)
            if near:
                for side, dy in ((0, -1), (1, 1)):
                    copies.append(send(edge1.at[kind, side], from_y1.at[kind, side], 0, dy))
        return first, rest

    def padded1(kind, width):
        below, above = pl.ds(HALO - width + 1, width - 1), pl.ds(0, width - 1)
        lower = joined(from_d1[kind, 2, below], from_d1[kind, 3, below])[1]
        upper = joined(from_d1[kind, 0, above], from_d1[kind, 1, above])[0]
        center = jnp.concatenate(joined(from_y1[kind, 0], from_y1[kind, 1]), 0)
        inside = [from_x1[kind, 1, HALO - width :], whole1[kind], from_x1[kind, 0, :width]]
        return jnp.concatenate(
            [jnp.concatenate(inside, 0), halo_rows(center, lower, upper)], 1
        )

    def fields_of(start, inside, right, left):
        halos = joined(right, left)
        return tuple(
            Strip(start, jnp.concatenate([cells, halo], 1)) for cells, halo in zip(inside, halos)
        )

    def right_of_strip(conc):
        cells = conc.cells
        return conc, Strip(conc.start, cells * cells * cells - (1.0 + STABILIZER) * cells)

    arrive(beside)
    level0 = Level(1.0, 1, 1)
    middle = fields_of(0, (conc, chem), from_y0[0], from_y0[1])
    mob_middle = Strip(0, mobility_of(middle[0].cells))
    coupling = Strip(1, level0.coupled(mob_middle.at(1, size - 1), level0.sums(mob_middle.cells)))
    level0.set(mob_middle, coupling)
    damp_middle = level0.damp
    right_middle = right_of_strip(middle[0])
    once_middle = level0.sweep(*middle, right_middle, 1, size - 1)
    both_middle = level0.sweep(*once_middle, right_middle, 2, size - 2)
    defect_middle = level0.residual(*both_middle, right_middle, 3, size - 3)

    arrive(outer)
    low_right = jnp.concatenate([from_d0[2][:1], from_d0[2]], 0)
    low_left = jnp.concatenate([from_d0[3][:1], from_d0[3]], 0)
    high_right = jnp.concatenate([from_d0[0], from_d0[0][-1:]], 0)
    high_left = jnp.concatenate([from_d0[1], from_d0[1][-1:]], 0)
    lows = fields_of(-HALO, (from_x0[1, 0], from_x0[1, 1]), low_right, low_left)
    highs = fields_of(size, (from_x0[0, 0], from_x0[0, 1]), high_right, high_left)
    fields = tuple(strips(*parts) for parts in zip(lows, middle, highs))
    mob_low, mob_high = (Strip(part[0].start, mobility_of(part[0].cells)) for part in (lows, highs))
    mob0 = strips(mob_low, mob_middle, mob_high)
    right_low, right_high = right_of_strip(lows[0]), right_of_strip(highs[0])
    right_side0 = tuple(strips(*parts) for parts in zip(right_low, right_middle, right_high))

    mob_x = pair_sum(pair_rows(mob0.at(-2, size + 2)), 1, 2) * 0.125
    mob1 = row_pairs(jnp.concatenate([mob_x, mob_x[:, 16:24]], 1))
    mob1_sum = near_sum(mob1, 1, 2)[:, :8]
    mob1 = mob1[1:-1, :8]
    even1 = iota((half, 8, 128), 2) % 2 == 0
    whole1[1] = jnp.where(even1, mob1, mob1_sum)
    mob1_waits, _ = swap1(1, HALO)
    pack2[1] = by_lane(twice_pair(pair_sum(pair_rows(mob1), 2, 2) * 0.125))
    mob2_waits = gather(1)

    def outer_coupling(low, high):
        near = level0.sums(mob0.at(low - 1, high + 1))
        return Strip(low, level0.coupled(mob0.at(low, high), near))

    coupling_low, coupling_high = outer_coupling(-3, 1), outer_coupling(size - 1, size + 3)
    level0.set(mob0, coupling_low)
    damp_low = level0.damp
    level0.set(mob0, coupling_high)
    level0.damp = strips(damp_low, damp_middle, level0.damp)
    level0.coupling = strips(coupling_low, coupling, coupling_high)

    def completed(now, before, low, high):
        inner = now[0].start, now[0].start + now[0].cells.shape[0]
        below = level0.sweep(*before, right_side0, low, inner[0])
        above = level0.sweep(*before, right_side0, inner[1], high)
        return tuple(strips(*parts) for parts in zip(below, now, above))

    once = completed(once_middle, fields, -3, size + 3)
    fields0 = completed(both_middle, once, -2, size + 2)
    below = level0.residual(*fields0, right_side0, 0, 3)
    above = level0.residual(*fields0, right_side0, size - 3, size)
    first, second = (
        jnp.concatenate(parts, 0)[:, :16] for parts in zip(below, defect_middle, above)
    )
    whole1[0] = jnp.where(even1, coarse(first, 1), coarse(second, 1))
    near_waits, far_waits = swap1(0, 2)

    arrive(mob1_waits)
    mob1, mob1_sum = spread(padded1(1, HALO), 1, 2)
    level1 = Level(0.25, 1, 2)
    level1.set(Strip(-HALO, mob1), Strip(-HALO, level1.coupled(mob1, mob1_sum)))
    arrive(near_waits)
    rhs1 = spread(padded1(0, 2), 1, 2)
    conc, chem = level1.step(*rhs1, -2)
    rhs1 = [Strip(-2, values) for values in rhs1]
    conc, chem = level1.sweep(conc, chem, rhs1, -1, half + 1)
    own = [
        twice_pair(pair_sum(pair_rows(values[:, :8]), 2, 2) * 0.125)
        for values in level1.residual(conc, chem, rhs1, 0, half)
    ]
    pack2[0] = jnp.where(iota((8, 128), 0) % 2 == 0, by_lane(own[0]), by_lane(own[1]))
    rhs2_waits = gather(0)

    arrive(far_waits)
    rhs1 = spread(padded1(0, HALO), 1, 2)
    conc, chem = level1.step(*rhs1, -HALO)
    rhs1 = [Strip(-HALO, values) for values in rhs1]
    fields1 = level1.sweep(conc, chem, rhs1, -3, half + 3)

    def by_row(values):
        zero, one = spread(values, 1, 2)
        zero, two = spread(zero, 2, 2)
        one, three = spread(one, 2, 2)
        together = jnp.stack([zero, one, two, three], 1)
        return together.reshape((nx * quarter,) + values.shape[1:])

    arrive(mob2_waits)
    mob2 = by_row(grid2[1, :, pl.ds(0, 4 * ny, stride=2)])
    mob3 = coarse(mob2, 4)
    level2, level3 = Level(0.0625, 1, 4, True), Level(0.015625, 1, 8, True)
    for level, mob in ((level2, mob2), (level3, mob3)):
        level.set(Strip(0, mob), Strip(0, level.coupled(mob, level.sums(mob))))

    arrive(rhs2_waits)
    rhs2 = [by_row(grid2[0, :, pl.ds(start, 4 * ny, stride=2)]) for start in (0, 1)]
    conc, chem = level2.step(*rhs2, 0)
    rhs2 = [Strip(0, values) for values in rhs2]
    conc, chem = level2.sweep(conc, chem, rhs2, 0, nx * quarter)
    rhs3 = [coarse(v, 4) for v in level2.residual(conc, chem, rhs2, 0, nx * quarter)]
    low_conc, low_chem = level3.step(*rhs3, 0)
    rhs3 = [Strip(0, values) for values in rhs3]
    low_conc, low_chem = level3.sweeps(COARSE - 1, low_conc, low_chem, rhs3)
    conc = Strip(0, conc.cells + twice(rows_twice(low_conc.cells)))
    chem = Strip(0, chem.cells + twice(rows_twice(low_chem.cells)))
    conc, chem = level2.sweeps(SWEEPS, conc, chem, rhs2)

    def around1(values):
        values = jnp.concatenate([values[-2:], values[: quarter + 2]], 0)
        values = rows_twice(values)
        low = iota((quarter + 4, 8, 128), 1) < 4
        beside = jnp.where(low, values[:, 8:16], values[:, -8:])
        return twice(jnp.concatenate([values[:, :8], beside], 1))[1:-1]

    conc, chem = (
        Strip(-3, old.cells + around1(new.cells)) for old, new in zip(fields1, (conc, chem))
    )
    conc, chem = level1.sweep(conc, chem, rhs1, -2, half + 2)
    conc, chem = level1.sweep(conc, chem, rhs1, -1, half + 1)

    def around0(values):
        doubled = rows_twice(values)
        low = iota((values.shape[0], 8, 128), 1) < 4
        beside = jnp.where(low, doubled[:, 16:24], doubled[:, 24:32])
        return twice(jnp.concatenate([doubled[:, :16], beside], 1))

    conc, chem = (
        Strip(-2, old.cells + around0(new.cells)) for old, new in zip(fields0, (conc, chem))
    )
    conc, chem = level0.sweep(conc, chem, right_side0, -1, size + 1)
    conc, chem = level0.sweep(conc, chem, right_side0, 0, size)
    conc_out[...] = conc.cells[:, :16]
    chem_out[...] = chem.cells[:, :16]
    for copy in started:
        copy.wait_send()


def gathered_cycle(nx, ny, conc_old, chem_old):
    size = conc_old.shape[0]
    half = size // 2
    copies = 10 + 8 + 14 + 2 * (nx * ny - 1)
    scratch = [
        conc_old.shape,
        conc_old.shape,
        (2, size, 8, 128),
        (2, 2, HALO, 16, 128),
        (2, size, 8, 128),
        (4, HALO - 1, 8, 128),
        (2, half, 8, 128),
        (2, 2, half // 2, 8, 128),
        (2, 2, HALO, 8, 128),
        (2, 2, half // 2, 8, 128),
        (2, 4, HALO, 8, 128),
        (2, 8, 128),
        (2, nx, ny * 8, 128),
        (2 * nx + half, 8 * ny, 128),
    ]
    shape = jax.ShapeDtypeStruct(conc_old.shape, jnp.float32)
    space = pl.BlockSpec(memory_space=pltpu.VMEM)
    away = pl.BlockSpec(memory_space=pl.ANY)
    return pl.pallas_call(
        functools.partial(cycle_kernel, nx, ny),
        out_shape=(shape, shape),
        in_specs=[away, away],
        out_specs=(space, space),
        scratch_shapes=[pltpu.VMEM(dims, jnp.float32) for dims in scratch]
        + [pltpu.SemaphoreType.DMA((count,)) for count in (2, copies, copies)],
        compiler_params=pltpu.CompilerParams(
            collective_id=0, has_side_effects=True, vmem_limit_bytes=60 * 1024 * 1024
        ),
    )(conc_old, chem_old)


def body(conc_old, chem_old):
    nx, ny = lax.axis_size("gx"), lax.axis_size("gy")
    if conc_old.shape == (16, 16, 128) and nx >= 3 and ny == 4 and nx * ny <= 16:
        return gathered_cycle(nx, ny, conc_old, chem_old)
    result = plain_solve(jnp.stack([conc_old, chem_old]))
    return (result[0], result[1])


def solution(mesh):
    in_specs = (P(("img", "gx"), "gy", None), P(("img", "gx"), "gy", None))
    out_specs = (P(("img", "gx"), "gy", None), P(("img", "gx"), "gy", None))
    return jax.shard_map(body, mesh=mesh, in_specs=in_specs, out_specs=out_specs, check_vma=False)
```

```python
import functools

import jax
import jax.numpy as jnp
from jax import lax
from jax.experimental import pallas as pl
from jax.experimental.pallas import tpu as pltpu
from jax.sharding import PartitionSpec as P

LEVELS = 4
SWEEPS = 2
COARSE = 6


TIME_STEP = 32.0
GRADIENT_ENERGY = 0.5
STABILIZER = 2.0
DAMPING = 0.7


def extended(cells, sides, width):
    for axis, dim in sides:
        count = lax.axis_size(axis)
        head = lax.slice_in_dim(cells, 0, width, axis=dim)
        tail = lax.slice_in_dim(cells, cells.shape[dim] - width, cells.shape[dim], axis=dim)
        cells = jnp.concatenate(
            [
                lax.ppermute(tail, axis, [(i, (i + 1) % count) for i in range(count)]),
                cells,
                lax.ppermute(head, axis, [((i + 1) % count, i) for i in range(count)]),
            ],
            axis=dim,
        )
    return cells


def mobility_of(concentration):
    return 0.1 + jnp.square(1.0 - concentration * concentration)


def right_of(concentration):
    return jnp.stack(
        [
            concentration,
            concentration * concentration * concentration - (1.0 + STABILIZER) * concentration,
        ]
    )


def face_weights(mob_padded, level_scale):
    middle = mob_padded[1:-1, 1:-1, :]
    half_scale = 0.5 * level_scale
    weights = (
        half_scale * (middle + mob_padded[2:, 1:-1, :]),
        half_scale * (middle + mob_padded[:-2, 1:-1, :]),
        half_scale * (middle + mob_padded[1:-1, 2:, :]),
        half_scale * (middle + mob_padded[1:-1, :-2, :]),
        half_scale * (middle + jnp.roll(middle, -1, axis=2)),
        half_scale * (middle + jnp.roll(middle, 1, axis=2)),
    )
    total_weight = weights[0] + weights[1] + weights[2] + weights[3] + weights[4] + weights[5]
    return (weights, total_weight)


def neighbour_list(padded, middle):
    return (
        padded[2:, 1:-1, :],
        padded[:-2, 1:-1, :],
        padded[1:-1, 2:, :],
        padded[1:-1, :-2, :],
        jnp.roll(middle, -1, axis=2),
        jnp.roll(middle, 1, axis=2),
    )


def apply_operator(padded, weights, level_scale):
    middle = padded[:, 1:-1, 1:-1, :]
    conc_near = neighbour_list(padded[0], middle[0])
    chem_near = neighbour_list(padded[1], middle[1])
    flux = weights[0] * (chem_near[0] - middle[1])
    for position in range(1, 6):
        flux = flux + weights[position] * (chem_near[position] - middle[1])
    laplace = (
        conc_near[0]
        + conc_near[1]
        + conc_near[2]
        + conc_near[3]
        + conc_near[4]
        + conc_near[5]
        - 6.0 * middle[0]
    )
    first_eq = middle[0] - TIME_STEP * flux
    second_eq = middle[1] - STABILIZER * middle[0] + GRADIENT_ENERGY * level_scale * laplace
    return jnp.stack([first_eq, second_eq])


def update(residual, total_weight, level_scale):
    diagonal = STABILIZER + 6.0 * GRADIENT_ENERGY * level_scale
    coupling = TIME_STEP * total_weight
    determinant = 1.0 + coupling * diagonal
    conc_step = (residual[0] - coupling * residual[1]) / determinant
    chem_step = (residual[1] + diagonal * residual[0]) / determinant
    return DAMPING * jnp.stack([conc_step, chem_step])


def sweep_once(padded, right_side, mob_padded, level_scale):
    weights, total_weight = face_weights(mob_padded, level_scale)
    residual = right_side - apply_operator(padded, weights, level_scale)
    return padded[:, 1:-1, 1:-1, :] + update(residual, total_weight, level_scale)


def defect(padded, right_side, mob_padded, level_scale):
    weights = face_weights(mob_padded, level_scale)[0]
    return right_side - apply_operator(padded, weights, level_scale)


def coarsen(values):
    dims_now = values.shape
    grouped = values.reshape(
        dims_now[:-3] + (dims_now[-3] // 2, 2, dims_now[-2] // 2, 2, dims_now[-1] // 2, 2)
    )
    return jnp.sum(grouped, axis=(-5, -3, -1)) * 0.125


def refine(values):
    for axis_pos in (-3, -2, -1):
        values = jnp.repeat(values, 2, axis=axis_pos)
    return values


def trim_rim(values, width):
    return values[..., width:-width, width:-width, :]


def field_rim(fields):
    return extended(fields, (("gx", 1), ("gy", 2)), 1)


def coarsest_solve(right_side, mobility, level_scale):
    mob_padded = extended(mobility, (("gx", 0), ("gy", 1)), 1)
    fields = update(right_side, face_weights(mob_padded, level_scale)[1], level_scale)
    for sweep_index in range(COARSE - 1):
        padded = extended(fields, (("gx", 1), ("gy", 2)), 1)
        fields = sweep_once(padded, right_side, mob_padded, level_scale)
    return fields


def plain_solve(start_fields):
    outer_fields = field_rim(start_fields)
    mob_outer = mobility_of(outer_fields[0])
    mobility = trim_rim(mob_outer, 1)
    level_data = []
    for level_index in range(LEVELS - 1):
        if level_index == 0:
            mob_padded = mob_outer
        else:
            mob_padded = extended(mobility, (("gx", 0), ("gy", 1)), 1)
        level_data.append((mob_padded, 0.25**level_index))
        mobility = coarsen(mobility)
    coarsest_scale = 0.25 ** (LEVELS - 1)

    def cycle_level(level_index, right_side):
        if level_index == LEVELS - 1:
            return coarsest_solve(right_side, mobility, coarsest_scale)
        mob_padded, level_scale = level_data[level_index]
        if level_index == 0:
            fields = sweep_once(outer_fields, right_side, mob_padded, level_scale)
        else:
            fields = update(right_side, face_weights(mob_padded, level_scale)[1], level_scale)
        fields = sweep_once(field_rim(fields), right_side, mob_padded, level_scale)
        residual = defect(field_rim(fields), right_side, mob_padded, level_scale)
        fields = fields + refine(cycle_level(level_index + 1, coarsen(residual)))
        for sweep_index in range(SWEEPS):
            fields = sweep_once(field_rim(fields), right_side, mob_padded, level_scale)
        return fields

    return cycle_level(0, right_of(start_fields[0]))


MESH = pl.DeviceIdType.MESH
HALO = 4
SIDES = (("lo", -1), ("hi", 1))
CORNERS = ((-1, -1), (-1, 1), (1, -1), (1, 1))


def iota(shape, dim):
    return lax.broadcasted_iota(jnp.int32, shape, dim)


def turn(values, shift, axis):
    size = values.shape[axis]
    return pltpu.roll(values, shift % size, axis)


def near_sum(values, row_step, lane_step, wrap=False):
    if wrap:
        middle = values
        total = jnp.concatenate([values[1:], values[:1]], 0) + jnp.concatenate(
            [values[-1:], values[:-1]], 0
        )
    else:
        middle = values[1:-1]
        total = values[2:] + values[:-2]
    total = total + (turn(middle, row_step, 1) + turn(middle, -row_step, 1))
    return total + (turn(middle, lane_step, 2) + turn(middle, -lane_step, 2))


def pair_sum(values, step, axis):
    low = (iota(values.shape, axis) // step) % 2 == 0
    return values + jnp.where(low, turn(values, -step, axis), turn(values, step, axis))


def pair_rows(values):
    grouped = values.reshape((values.shape[0] // 2, 2) + values.shape[1:])
    return grouped[:, 0] + grouped[:, 1]


def twice(values):
    return jnp.concatenate([values[i // 2 : i // 2 + 1] for i in range(2 * values.shape[0])], 0)


class Strip:
    def __init__(self, start, cells):
        self.start, self.cells = start, cells

    def at(self, low, high):
        return self.cells[low - self.start : high - self.start]


def strips(*parts):
    return Strip(parts[0].start, jnp.concatenate([part.cells for part in parts], 0))


class Level:
    def __init__(self, scale, row_step, lane_step, wrap=False):
        self.scale = scale
        self.row_step, self.lane_step, self.wrap = row_step, lane_step, wrap
        self.half = 0.5 * TIME_STEP * scale
        self.diagonal = STABILIZER + 6.0 * GRADIENT_ENERGY * scale
        self.mob = self.coupling = self.damp = None

    def set(self, mob, coupling):
        self.mob = mob
        self.coupling = coupling
        self.damp = Strip(coupling.start, DAMPING / (1.0 + coupling.cells * self.diagonal))
        return self

    def sums(self, values):
        return near_sum(values, self.row_step, self.lane_step, self.wrap)

    def coupled(self, mob, mob_sum):
        return self.half * (6.0 * mob + mob_sum)

    def residual(self, conc, chem, right, low, high):
        rim = 0 if self.wrap else 1
        c, u, mob = conc.at(low, high), chem.at(low, high), self.mob.at(low, high)
        near_chem = chem.at(low - rim, high + rim)
        carried = self.mob.at(low - rim, high + rim) * near_chem
        first = (
            right[0].at(low, high)
            - c
            + self.half * (mob * self.sums(near_chem) + self.sums(carried))
            - self.coupling.at(low, high) * u
        )
        near = self.sums(conc.at(low - rim, high + rim)) - 6.0 * c
        second = (
            right[1].at(low, high)
            - u
            + STABILIZER * c
            - (GRADIENT_ENERGY * self.scale) * near
        )
        return first, second

    def step(self, first, second, low):
        high = low + first.shape[0]
        damp = self.damp.at(low, high)
        coupling = self.coupling.at(low, high)
        conc_step = damp * (first - coupling * second)
        return Strip(low, conc_step), Strip(low, damp * (second + self.diagonal * first))

    def sweep(self, conc, chem, right, low, high):
        dc, du = self.step(*self.residual(conc, chem, right, low, high), low)
        return Strip(low, conc.at(low, high) + dc.cells), Strip(low, chem.at(low, high) + du.cells)

    def sweeps(self, count, conc, chem, right):
        size = conc.cells.shape[0]

        def once(_, now):
            new = self.sweep(Strip(0, now[0]), Strip(0, now[1]), right, 0, size)
            return new[0].cells, new[1].cells

        now = lax.fori_loop(0, count, once, (conc.cells, chem.cells))
        return Strip(0, now[0]), Strip(0, now[1])


def split_halves(first, second, first_high, second_high):
    low = iota(first.shape, 1) < 4
    first = turn(first, 4, 1) if first_high else first
    second = second if second_high else turn(second, 4, 1)
    return jnp.where(low, first, second)


def cycle_kernel(nx, ny, own, result, *scratch):
    (
        edge0,
        from_x0,
        from_y0,
        from_d0,
        whole1,
        edge1,
        from_x1,
        from_y1,
        from_d1,
        pack2,
        grid2,
        rows_buf,
        send_sem,
        recv_sem,
        spread_sem,
    ) = scratch
    img, gx, gy = lax.axis_index("img"), lax.axis_index("gx"), lax.axis_index("gy")
    x_at = [lax.rem(gx + dx, nx) for dx in range(nx)]
    y_at = [lax.rem(gy + dy, ny) for dy in range(ny)]

    def at(dx, dy):
        return (img, x_at[dx % nx], y_at[dy % ny])

    peers = [(dx, dy) for dx in [*range(1, nx), 0] for dy in range(ny) if (dx, dy) != (0, 0)]
    barrier = pltpu.get_barrier_semaphore()
    for dx, dy in peers:
        pl.semaphore_signal(barrier, inc=1, device_id=at(dx, dy), device_id_type=MESH)

    used = [0]

    def send(src, dst, dx, dy):
        index = used[0]
        used[0] += 1
        copy = pltpu.make_async_remote_copy(
            src_ref=src,
            dst_ref=dst,
            send_sem=send_sem.at[index],
            recv_sem=recv_sem.at[index],
            device_id=at(dx, dy),
            device_id_type=MESH,
        )
        copy.start()
        return copy

    def arrive(copies):
        for copy in copies:
            copy.wait_recv()

    size = own.shape[1]
    half = size // 2
    quarter = half // 2
    conc, chem = own[0], own[1]
    edge0[0] = split_halves(conc[:, :8], chem[:, :8], False, False)
    edge0[1] = split_halves(conc[:, -8:], chem[:, -8:], True, True)
    pl.semaphore_wait(barrier, len(peers))

    outer, beside = [], []
    for side, dx in ((0, -1), (1, 1)):
        rows = pl.ds(0, HALO) if dx < 0 else pl.ds(size - HALO, HALO)
        outer.append(send(own.at[:, rows], from_x0.at[side], dx, 0))
    for side, dy in ((0, -1), (1, 1)):
        beside.append(send(edge0.at[side], from_y0.at[side], 0, dy))
    for place, (dx, dy) in enumerate(CORNERS):
        rows = pl.ds(0, HALO - 1) if dx < 0 else pl.ds(size - HALO + 1, HALO - 1)
        outer.append(send(edge0.at[(dy + 1) // 2, rows], from_d0.at[place], dx, dy))

    def halo_rows(center, lower, upper):
        return jnp.concatenate([lower[:1], lower, center, upper, upper[-1:]], 0)

    def joined(right, left):
        low = iota(right.shape, 1) < 4
        return jnp.where(low, right, turn(left, 4, 1)), jnp.where(low, turn(right, 4, 1), left)

    def row_pairs(values):
        count, rows = values.shape[:2]
        rows_buf[:count, :rows] = values
        return (
            rows_buf[:count, pl.ds(0, rows // 2, stride=2)]
            + rows_buf[:count, pl.ds(1, rows // 2, stride=2)]
        )

    def rows_twice(values):
        count, rows = values.shape[:2]
        rows_buf[:count, pl.ds(0, rows, stride=2)] = values
        rows_buf[:count, pl.ds(1, rows, stride=2)] = values
        return rows_buf[:count, : 2 * rows]

    def coarse(values, lane_step):
        return row_pairs(pair_sum(pair_rows(values), lane_step, 2) * 0.125)

    def spread(values, step, axis):
        low = (iota(values.shape, axis) // step) % 2 == 0
        return (
            jnp.where(low, values, turn(values, step, axis)),
            jnp.where(low, turn(values, -step, axis), values),
        )

    def by_lane(values):
        lane = iota((8, 128), 1) % 4
        return jnp.where(
            lane < 2,
            jnp.where(lane == 0, values[0], values[1]),
            jnp.where(lane == 2, values[2], values[3]),
        )

    def twice_pair(values):
        return pair_sum(values, 1, 1)

    def gather(kind):
        for dx, dy in peers:
            rows = pl.ds(8 * ((ny - dy) % ny), 8)
            index = 2 * kind + (dx == 0)
            pltpu.make_async_remote_copy(
                src_ref=pack2.at[kind],
                dst_ref=grid2.at[kind, (nx - dx) % nx, rows],
                send_sem=spread_sem.at[0, index],
                recv_sem=spread_sem.at[1, index],
                device_id=at(dx, dy),
                device_id_type=MESH,
            ).start()
        grid2[kind, 0, :8] = pack2[kind]
        views = grid2.at[kind, pl.ds(1, nx - 1)], grid2.at[kind, 0, pl.ds(8, 8 * ny - 8)]
        return [
            pltpu.make_async_remote_copy(
                src_ref=view,
                dst_ref=view,
                send_sem=spread_sem.at[0, 2 * kind + index],
                recv_sem=spread_sem.at[1, 2 * kind + index],
                device_id=at(1 - index, index),
                device_id_type=MESH,
            )
            for index, view in enumerate(views)
        ]

    def drain(copies):
        for copy in copies:
            copy.wait_send()

    def swap1(kind, inner):
        first, rest = [], []
        edge1[kind, 0] = split_halves(whole1[kind, :4], whole1[kind, 4:], False, False)
        edge1[kind, 1] = split_halves(whole1[kind, :4], whole1[kind, 4:], True, True)

        def move(copies, src, dst, start, count, dx, dy, shift=0):
            if count > 0:
                source = src.at[pl.ds(start + shift, count)]
                copies.append(send(source, dst.at[pl.ds(start, count)], dx, dy))

        for copies in (first, rest):
            near = copies is first
            for side, dx in ((0, -1), (1, 1)):
                count = inner if near else HALO - inner
                start = 0 if (dx < 0) == near else HALO - count
                shift = 0 if dx < 0 else half - HALO
                move(copies, whole1.at[kind], from_x1.at[kind, side], start, count, dx, 0, shift)
            for place, (dx, dy) in enumerate(CORNERS):
                count = inner - 1 if near else HALO - inner
                if dx < 0:
                    start = 0 if near else inner - 1
                else:
                    start = HALO - inner + 1 if near else 1
                source = edge1.at[kind, (dy + 1) // 2]
                move(copies, source, from_d1.at[kind, place], start, count, dx, dy)
            if near:
                for side, dy in ((0, -1), (1, 1)):
                    copies.append(send(edge1.at[kind, side], from_y1.at[kind, side], 0, dy))
        return first, rest

    def padded1(kind, width):
        below, above = pl.ds(HALO - width + 1, width - 1), pl.ds(0, width - 1)
        lower = joined(from_d1[kind, 2, below], from_d1[kind, 3, below])[1]
        upper = joined(from_d1[kind, 0, above], from_d1[kind, 1, above])[0]
        center = jnp.concatenate(joined(from_y1[kind, 0], from_y1[kind, 1]), 0)
        inside = [from_x1[kind, 1, HALO - width :], whole1[kind], from_x1[kind, 0, :width]]
        return jnp.concatenate(
            [jnp.concatenate(inside, 0), halo_rows(center, lower, upper)], 1
        )

    def fields_of(start, inside, right, left):
        halos = joined(right, left)
        return tuple(
            Strip(start, jnp.concatenate([cells, halo], 1)) for cells, halo in zip(inside, halos)
        )

    def right_of_strip(conc):
        cells = conc.cells
        return conc, Strip(conc.start, cells * cells * cells - (1.0 + STABILIZER) * cells)

    mob1 = coarse(mobility_of(conc), 1)
    pack2[1] = by_lane(twice_pair(pair_sum(pair_rows(mob1), 2, 2) * 0.125))
    mob2_waits = gather(1)

    arrive(beside)
    level0 = Level(1.0, 1, 1)
    middle = fields_of(0, (conc, chem), from_y0[0], from_y0[1])
    mob_middle = Strip(0, mobility_of(middle[0].cells))
    coupling = Strip(1, level0.coupled(mob_middle.at(1, size - 1), level0.sums(mob_middle.cells)))
    level0.set(mob_middle, coupling)
    damp_middle = level0.damp
    right_middle = right_of_strip(middle[0])
    once_middle = level0.sweep(*middle, right_middle, 1, size - 1)
    both_middle = level0.sweep(*once_middle, right_middle, 2, size - 2)
    defect_middle = level0.residual(*both_middle, right_middle, 3, size - 3)

    arrive(outer)
    low_right = jnp.concatenate([from_d0[2][:1], from_d0[2]], 0)
    low_left = jnp.concatenate([from_d0[3][:1], from_d0[3]], 0)
    high_right = jnp.concatenate([from_d0[0], from_d0[0][-1:]], 0)
    high_left = jnp.concatenate([from_d0[1], from_d0[1][-1:]], 0)
    lows = fields_of(-HALO, (from_x0[1, 0], from_x0[1, 1]), low_right, low_left)
    highs = fields_of(size, (from_x0[0, 0], from_x0[0, 1]), high_right, high_left)
    fields = tuple(strips(*parts) for parts in zip(lows, middle, highs))
    mob_low, mob_high = (Strip(part[0].start, mobility_of(part[0].cells)) for part in (lows, highs))
    mob0 = strips(mob_low, mob_middle, mob_high)
    right_low, right_high = right_of_strip(lows[0]), right_of_strip(highs[0])
    right_side0 = tuple(strips(*parts) for parts in zip(right_low, right_middle, right_high))

    mob_x = pair_sum(pair_rows(mob0.at(-2, size + 2)), 1, 2) * 0.125
    mob1 = row_pairs(jnp.concatenate([mob_x, mob_x[:, 16:24]], 1))
    mob1_sum = near_sum(mob1, 1, 2)[:, :8]
    mob1 = mob1[1:-1, :8]
    even1 = iota((half, 8, 128), 2) % 2 == 0
    whole1[1] = jnp.where(even1, mob1, mob1_sum)
    mob1_waits, _ = swap1(1, HALO)

    def outer_coupling(low, high):
        near = level0.sums(mob0.at(low - 1, high + 1))
        return Strip(low, level0.coupled(mob0.at(low, high), near))

    coupling_low, coupling_high = outer_coupling(-3, 1), outer_coupling(size - 1, size + 3)
    level0.set(mob0, coupling_low)
    damp_low = level0.damp
    level0.set(mob0, coupling_high)
    level0.damp = strips(damp_low, damp_middle, level0.damp)
    level0.coupling = strips(coupling_low, coupling, coupling_high)

    def completed(now, before, low, high):
        inner = now[0].start, now[0].start + now[0].cells.shape[0]
        below = level0.sweep(*before, right_side0, low, inner[0])
        above = level0.sweep(*before, right_side0, inner[1], high)
        return tuple(strips(*parts) for parts in zip(below, now, above))

    once = completed(once_middle, fields, -3, size + 3)
    fields0 = completed(both_middle, once, -2, size + 2)
    below = level0.residual(*fields0, right_side0, 0, 3)
    above = level0.residual(*fields0, right_side0, size - 3, size)
    first, second = (
        jnp.concatenate(parts, 0)[:, :16] for parts in zip(below, defect_middle, above)
    )
    whole1[0] = jnp.where(even1, coarse(first, 1), coarse(second, 1))
    near_waits, far_waits = swap1(0, 2)

    arrive(mob1_waits)
    mob1, mob1_sum = spread(padded1(1, HALO), 1, 2)
    level1 = Level(0.25, 1, 2)
    level1.set(Strip(-HALO, mob1), Strip(-HALO, level1.coupled(mob1, mob1_sum)))
    drain(outer + beside + mob1_waits)
    def by_row(values):
        zero, one = spread(values, 1, 2)
        zero, two = spread(zero, 2, 2)
        one, three = spread(one, 2, 2)
        together = jnp.stack([zero, one, two, three], 1)
        return together.reshape((nx * quarter,) + values.shape[1:])

    arrive(mob2_waits)
    mob2 = by_row(grid2[1, :, pl.ds(0, 4 * ny, stride=2)])
    mob3 = coarse(mob2, 4)
    level2, level3 = Level(0.0625, 1, 4, True), Level(0.015625, 1, 8, True)
    for level, mob in ((level2, mob2), (level3, mob3)):
        level.set(Strip(0, mob), Strip(0, level.coupled(mob, level.sums(mob))))

    drain(mob2_waits)
    arrive(near_waits)
    rhs1 = spread(padded1(0, 2), 1, 2)
    conc, chem = level1.step(*rhs1, -2)
    rhs1 = [Strip(-2, values) for values in rhs1]
    conc, chem = level1.sweep(conc, chem, rhs1, -1, half + 1)
    own = [
        twice_pair(pair_sum(pair_rows(values[:, :8]), 2, 2) * 0.125)
        for values in level1.residual(conc, chem, rhs1, 0, half)
    ]
    pack2[0] = jnp.where(iota((8, 128), 0) % 2 == 0, by_lane(own[0]), by_lane(own[1]))
    rhs2_waits = gather(0)

    arrive(far_waits)
    rhs1 = spread(padded1(0, HALO), 1, 2)
    conc, chem = level1.step(*rhs1, -HALO)
    rhs1 = [Strip(-HALO, values) for values in rhs1]
    fields1 = level1.sweep(conc, chem, rhs1, -3, half + 3)

    drain(near_waits + far_waits)
    arrive(rhs2_waits)
    rhs2 = [by_row(grid2[0, :, pl.ds(start, 4 * ny, stride=2)]) for start in (0, 1)]
    conc, chem = level2.step(*rhs2, 0)
    rhs2 = [Strip(0, values) for values in rhs2]
    conc, chem = level2.sweep(conc, chem, rhs2, 0, nx * quarter)
    rhs3 = [coarse(v, 4) for v in level2.residual(conc, chem, rhs2, 0, nx * quarter)]
    low_conc, low_chem = level3.step(*rhs3, 0)
    rhs3 = [Strip(0, values) for values in rhs3]
    low_conc, low_chem = level3.sweeps(COARSE - 1, low_conc, low_chem, rhs3)
    conc = Strip(0, conc.cells + twice(rows_twice(low_conc.cells)))
    chem = Strip(0, chem.cells + twice(rows_twice(low_chem.cells)))
    conc, chem = level2.sweeps(SWEEPS, conc, chem, rhs2)

    def around1(values):
        values = jnp.concatenate([values[-2:], values[: quarter + 2]], 0)
        values = rows_twice(values)
        low = iota((quarter + 4, 8, 128), 1) < 4
        beside = jnp.where(low, values[:, 8:16], values[:, -8:])
        return twice(jnp.concatenate([values[:, :8], beside], 1))[1:-1]

    conc, chem = (
        Strip(-3, old.cells + around1(new.cells)) for old, new in zip(fields1, (conc, chem))
    )
    conc, chem = level1.sweep(conc, chem, rhs1, -2, half + 2)
    conc, chem = level1.sweep(conc, chem, rhs1, -1, half + 1)

    def around0(values):
        doubled = rows_twice(values)
        low = iota((values.shape[0], 8, 128), 1) < 4
        beside = jnp.where(low, doubled[:, 16:24], doubled[:, 24:32])
        return twice(jnp.concatenate([doubled[:, :16], beside], 1))

    conc, chem = (
        Strip(-2, old.cells + around0(new.cells)) for old, new in zip(fields0, (conc, chem))
    )
    conc, chem = level0.sweep(conc, chem, right_side0, -1, size + 1)
    conc, chem = level0.sweep(conc, chem, right_side0, 0, size)
    result[0] = conc.cells[:, :16]
    result[1] = chem.cells[:, :16]
    drain(rhs2_waits)


def gathered_cycle(nx, ny, fields):
    size = fields.shape[1]
    half = size // 2
    copies = 8 + 8 + 14
    scratch = [
        (2, size, 8, 128),
        (2, 2, HALO, 16, 128),
        (2, size, 8, 128),
        (4, HALO - 1, 8, 128),
        (2, half, 8, 128),
        (2, 2, half // 2, 8, 128),
        (2, 2, HALO, 8, 128),
        (2, 2, half // 2, 8, 128),
        (2, 4, HALO, 8, 128),
        (2, 8, 128),
        (2, nx, ny * 8, 128),
        (2 * nx + half, 8 * ny, 128),
    ]
    shape = jax.ShapeDtypeStruct(fields.shape, jnp.float32)
    space = pl.BlockSpec(memory_space=pltpu.VMEM)
    return pl.pallas_call(
        functools.partial(cycle_kernel, nx, ny),
        out_shape=shape,
        in_specs=[space],
        out_specs=space,
        scratch_shapes=[pltpu.VMEM(dims, jnp.float32) for dims in scratch]
        + [pltpu.SemaphoreType.DMA((count,)) for count in (copies, copies)]
        + [pltpu.SemaphoreType.DMA((2, 4))],
        compiler_params=pltpu.CompilerParams(
            collective_id=0, has_side_effects=True, vmem_limit_bytes=32 * 1024 * 1024
        ),
    )(fields)


def body(conc_old, chem_old):
    nx, ny = lax.axis_size("gx"), lax.axis_size("gy")
    if conc_old.shape == (16, 16, 128) and nx >= 3 and ny == 4 and nx * ny <= 16:
        result = gathered_cycle(nx, ny, jnp.stack([conc_old, chem_old]))
    else:
        result = plain_solve(jnp.stack([conc_old, chem_old]))
    return (result[0], result[1])


def solution(mesh):
    in_specs = (P(("img", "gx"), "gy", None), P(("img", "gx"), "gy", None))
    out_specs = (P(("img", "gx"), "gy", None), P(("img", "gx"), "gy", None))
    return jax.shard_map(body, mesh=mesh, in_specs=in_specs, out_specs=out_specs, check_vma=False)
```

```python
import functools

import jax
import jax.numpy as jnp
from jax import lax
from jax.experimental import pallas as pl
from jax.experimental.pallas import tpu as pltpu
from jax.sharding import PartitionSpec as P

LEVELS = 4
SWEEPS = 2
COARSE = 6


TIME_STEP = 32.0
GRADIENT_ENERGY = 0.5
STABILIZER = 2.0
DAMPING = 0.7


def extended(cells, sides, width):
    for axis, dim in sides:
        count = lax.axis_size(axis)
        head = lax.slice_in_dim(cells, 0, width, axis=dim)
        tail = lax.slice_in_dim(cells, cells.shape[dim] - width, cells.shape[dim], axis=dim)
        cells = jnp.concatenate(
            [
                lax.ppermute(tail, axis, [(i, (i + 1) % count) for i in range(count)]),
                cells,
                lax.ppermute(head, axis, [((i + 1) % count, i) for i in range(count)]),
            ],
            axis=dim,
        )
    return cells


def mobility_of(concentration):
    return 0.1 + jnp.square(1.0 - concentration * concentration)


def right_of(concentration):
    return jnp.stack(
        [
            concentration,
            concentration * concentration * concentration - (1.0 + STABILIZER) * concentration,
        ]
    )


def face_weights(mob_padded, level_scale):
    middle = mob_padded[1:-1, 1:-1, :]
    half_scale = 0.5 * level_scale
    weights = (
        half_scale * (middle + mob_padded[2:, 1:-1, :]),
        half_scale * (middle + mob_padded[:-2, 1:-1, :]),
        half_scale * (middle + mob_padded[1:-1, 2:, :]),
        half_scale * (middle + mob_padded[1:-1, :-2, :]),
        half_scale * (middle + jnp.roll(middle, -1, axis=2)),
        half_scale * (middle + jnp.roll(middle, 1, axis=2)),
    )
    total_weight = weights[0] + weights[1] + weights[2] + weights[3] + weights[4] + weights[5]
    return (weights, total_weight)


def neighbour_list(padded, middle):
    return (
        padded[2:, 1:-1, :],
        padded[:-2, 1:-1, :],
        padded[1:-1, 2:, :],
        padded[1:-1, :-2, :],
        jnp.roll(middle, -1, axis=2),
        jnp.roll(middle, 1, axis=2),
    )


def apply_operator(padded, weights, level_scale):
    middle = padded[:, 1:-1, 1:-1, :]
    conc_near = neighbour_list(padded[0], middle[0])
    chem_near = neighbour_list(padded[1], middle[1])
    flux = weights[0] * (chem_near[0] - middle[1])
    for position in range(1, 6):
        flux = flux + weights[position] * (chem_near[position] - middle[1])
    laplace = (
        conc_near[0]
        + conc_near[1]
        + conc_near[2]
        + conc_near[3]
        + conc_near[4]
        + conc_near[5]
        - 6.0 * middle[0]
    )
    first_eq = middle[0] - TIME_STEP * flux
    second_eq = middle[1] - STABILIZER * middle[0] + GRADIENT_ENERGY * level_scale * laplace
    return jnp.stack([first_eq, second_eq])


def update(residual, total_weight, level_scale):
    diagonal = STABILIZER + 6.0 * GRADIENT_ENERGY * level_scale
    coupling = TIME_STEP * total_weight
    determinant = 1.0 + coupling * diagonal
    conc_step = (residual[0] - coupling * residual[1]) / determinant
    chem_step = (residual[1] + diagonal * residual[0]) / determinant
    return DAMPING * jnp.stack([conc_step, chem_step])


def sweep_once(padded, right_side, mob_padded, level_scale):
    weights, total_weight = face_weights(mob_padded, level_scale)
    residual = right_side - apply_operator(padded, weights, level_scale)
    return padded[:, 1:-1, 1:-1, :] + update(residual, total_weight, level_scale)


def defect(padded, right_side, mob_padded, level_scale):
    weights = face_weights(mob_padded, level_scale)[0]
    return right_side - apply_operator(padded, weights, level_scale)


def coarsen(values):
    dims_now = values.shape
    grouped = values.reshape(
        dims_now[:-3] + (dims_now[-3] // 2, 2, dims_now[-2] // 2, 2, dims_now[-1] // 2, 2)
    )
    return jnp.sum(grouped, axis=(-5, -3, -1)) * 0.125


def refine(values):
    for axis_pos in (-3, -2, -1):
        values = jnp.repeat(values, 2, axis=axis_pos)
    return values


def trim_rim(values, width):
    return values[..., width:-width, width:-width, :]


def field_rim(fields):
    return extended(fields, (("gx", 1), ("gy", 2)), 1)


def coarsest_solve(right_side, mobility, level_scale):
    mob_padded = extended(mobility, (("gx", 0), ("gy", 1)), 1)
    fields = update(right_side, face_weights(mob_padded, level_scale)[1], level_scale)
    for sweep_index in range(COARSE - 1):
        padded = extended(fields, (("gx", 1), ("gy", 2)), 1)
        fields = sweep_once(padded, right_side, mob_padded, level_scale)
    return fields


def plain_solve(start_fields):
    outer_fields = field_rim(start_fields)
    mob_outer = mobility_of(outer_fields[0])
    mobility = trim_rim(mob_outer, 1)
    level_data = []
    for level_index in range(LEVELS - 1):
        if level_index == 0:
            mob_padded = mob_outer
        else:
            mob_padded = extended(mobility, (("gx", 0), ("gy", 1)), 1)
        level_data.append((mob_padded, 0.25**level_index))
        mobility = coarsen(mobility)
    coarsest_scale = 0.25 ** (LEVELS - 1)

    def cycle_level(level_index, right_side):
        if level_index == LEVELS - 1:
            return coarsest_solve(right_side, mobility, coarsest_scale)
        mob_padded, level_scale = level_data[level_index]
        if level_index == 0:
            fields = sweep_once(outer_fields, right_side, mob_padded, level_scale)
        else:
            fields = update(right_side, face_weights(mob_padded, level_scale)[1], level_scale)
        fields = sweep_once(field_rim(fields), right_side, mob_padded, level_scale)
        residual = defect(field_rim(fields), right_side, mob_padded, level_scale)
        fields = fields + refine(cycle_level(level_index + 1, coarsen(residual)))
        for sweep_index in range(SWEEPS):
            fields = sweep_once(field_rim(fields), right_side, mob_padded, level_scale)
        return fields

    return cycle_level(0, right_of(start_fields[0]))


MESH = pl.DeviceIdType.MESH
HALO = 4
SIDES = (("lo", -1), ("hi", 1))
CORNERS = ((-1, -1), (-1, 1), (1, -1), (1, 1))


def iota(shape, dim):
    return lax.broadcasted_iota(jnp.int32, shape, dim)


def turn(values, shift, axis):
    size = values.shape[axis]
    return pltpu.roll(values, shift % size, axis)


def near_sum(values, row_step, lane_step):
    middle = values[1:-1]
    total = values[2:] + values[:-2]
    total = total + (turn(middle, row_step, 1) + turn(middle, -row_step, 1))
    return total + (turn(middle, lane_step, 2) + turn(middle, -lane_step, 2))


def pair_sum(values, step, axis):
    low = (iota(values.shape, axis) // step) % 2 == 0
    return values + jnp.where(low, turn(values, -step, axis), turn(values, step, axis))


def pair_rows(values):
    grouped = values.reshape((values.shape[0] // 2, 2) + values.shape[1:])
    return grouped[:, 0] + grouped[:, 1]


def twice(values):
    return jnp.concatenate([values[i // 2 : i // 2 + 1] for i in range(2 * values.shape[0])], 0)


class Strip:
    def __init__(self, start, cells):
        self.start, self.cells = start, cells

    def at(self, low, high):
        return self.cells[low - self.start : high - self.start]


def strips(*parts):
    return Strip(parts[0].start, jnp.concatenate([part.cells for part in parts], 0))


def wrapped(strip):
    cells = strip.cells
    return Strip(strip.start - 1, jnp.concatenate([cells[-1:], cells, cells[:1]], 0))


class Level:
    def __init__(self, scale, row_step, lane_step, layers, wrap=False):
        self.scale, self.layers = scale, layers
        self.row_step, self.lane_step, self.wrap = row_step, lane_step, wrap
        self.half = 0.5 * TIME_STEP * scale
        self.diagonal = STABILIZER + 6.0 * GRADIENT_ENERGY * scale
        self.mob = self.coupling = self.damp = None

    def pieces(self, work, low, high):
        parts = [
            work(at, min(at + self.layers, high)) for at in range(low, high, self.layers)
        ]
        return tuple(Strip(low, jnp.concatenate(cells, 0)) for cells in zip(*parts))

    def sums(self, values):
        return near_sum(values, self.row_step, self.lane_step)

    def setup(self, mob, low, high, mob_sum=None):
        def work(low, high):
            near = self.sums(mob.at(low - 1, high + 1)) if mob_sum is None else mob_sum.at(low, high)
            coupling = self.half * (6.0 * mob.at(low, high) + near)
            return coupling, DAMPING / (1.0 + coupling * self.diagonal)

        self.mob = mob
        self.coupling, self.damp = self.pieces(work, low, high)
        return self.coupling, self.damp

    def defect(self, conc, chem, right, low, high):
        c, u, mob = conc.at(low, high), chem.at(low, high), self.mob.at(low, high)
        near_chem = chem.at(low - 1, high + 1)
        carried = self.mob.at(low - 1, high + 1) * near_chem
        first = (
            right[0].at(low, high)
            - c
            + self.half * (mob * self.sums(near_chem) + self.sums(carried))
            - self.coupling.at(low, high) * u
        )
        near = self.sums(conc.at(low - 1, high + 1)) - 6.0 * c
        second = (
            right[1].at(low, high)
            - u
            + STABILIZER * c
            - (GRADIENT_ENERGY * self.scale) * near
        )
        return first, second

    def change(self, first, second, low, high):
        damp = self.damp.at(low, high)
        coupling = self.coupling.at(low, high)
        return damp * (first - coupling * second), damp * (second + self.diagonal * first)

    def residual(self, conc, chem, right, low, high):
        if self.wrap:
            conc, chem = wrapped(conc), wrapped(chem)
        parts = self.pieces(lambda *at: self.defect(conc, chem, right, *at), low, high)
        return tuple(part.cells for part in parts)

    def step(self, right, low, high):
        def work(low, high):
            return self.change(right[0].at(low, high), right[1].at(low, high), low, high)

        return self.pieces(work, low, high)

    def sweep(self, conc, chem, right, low, high):
        if self.wrap:
            conc, chem = wrapped(conc), wrapped(chem)

        def work(low, high):
            dc, du = self.change(*self.defect(conc, chem, right, low, high), low, high)
            return conc.at(low, high) + dc, chem.at(low, high) + du

        return self.pieces(work, low, high)

    def sweeps(self, count, conc, chem, right):
        size = conc.cells.shape[0]

        def once(_, now):
            new = self.sweep(Strip(0, now[0]), Strip(0, now[1]), right, 0, size)
            return new[0].cells, new[1].cells

        now = lax.fori_loop(0, count, once, (conc.cells, chem.cells))
        return Strip(0, now[0]), Strip(0, now[1])


def split_halves(first, second, first_high, second_high):
    low = iota(first.shape, 1) < 4
    first = turn(first, 4, 1) if first_high else first
    second = second if second_high else turn(second, 4, 1)
    return jnp.where(low, first, second)


def cycle_kernel(nx, ny, own, result, *scratch):
    (
        edge0,
        from_x0,
        from_y0,
        from_d0,
        whole1,
        edge1,
        from_x1,
        from_y1,
        from_d1,
        pack2,
        grid2,
        rows_buf,
        send_sem,
        recv_sem,
        spread_sem,
    ) = scratch
    img, gx, gy = lax.axis_index("img"), lax.axis_index("gx"), lax.axis_index("gy")
    x_at = [lax.rem(gx + dx, nx) for dx in range(nx)]
    y_at = [lax.rem(gy + dy, ny) for dy in range(ny)]

    def at(dx, dy):
        return (img, x_at[dx % nx], y_at[dy % ny])

    peers = [(dx, dy) for dx in [*range(1, nx), 0] for dy in range(ny) if (dx, dy) != (0, 0)]
    barrier = pltpu.get_barrier_semaphore()
    for dx, dy in peers:
        pl.semaphore_signal(barrier, inc=1, device_id=at(dx, dy), device_id_type=MESH)

    used = [0]

    def send(src, dst, dx, dy):
        index = used[0]
        used[0] += 1
        copy = pltpu.make_async_remote_copy(
            src_ref=src,
            dst_ref=dst,
            send_sem=send_sem.at[index],
            recv_sem=recv_sem.at[index],
            device_id=at(dx, dy),
            device_id_type=MESH,
        )
        copy.start()
        return copy

    def arrive(copies):
        for copy in copies:
            copy.wait_recv()

    size = own.shape[1]
    half = size // 2
    quarter = half // 2
    conc, chem = own[0], own[1]
    edge0[0] = split_halves(conc[:, :8], chem[:, :8], False, False)
    edge0[1] = split_halves(conc[:, -8:], chem[:, -8:], True, True)
    pl.semaphore_wait(barrier, len(peers))

    outer, beside = [], []
    for side, dx in ((0, -1), (1, 1)):
        rows = pl.ds(0, HALO) if dx < 0 else pl.ds(size - HALO, HALO)
        outer.append(send(own.at[:, rows], from_x0.at[side], dx, 0))
    for side, dy in ((0, -1), (1, 1)):
        beside.append(send(edge0.at[side], from_y0.at[side], 0, dy))
    for place, (dx, dy) in enumerate(CORNERS):
        rows = pl.ds(0, HALO - 1) if dx < 0 else pl.ds(size - HALO + 1, HALO - 1)
        outer.append(send(edge0.at[(dy + 1) // 2, rows], from_d0.at[place], dx, dy))

    def halo_rows(center, lower, upper):
        return jnp.concatenate([lower[:1], lower, center, upper, upper[-1:]], 0)

    def joined(right, left):
        low = iota(right.shape, 1) < 4
        return jnp.where(low, right, turn(left, 4, 1)), jnp.where(low, turn(right, 4, 1), left)

    def row_pairs(values):
        count, rows = values.shape[:2]
        rows_buf[:count, :rows] = values
        return (
            rows_buf[:count, pl.ds(0, rows // 2, stride=2)]
            + rows_buf[:count, pl.ds(1, rows // 2, stride=2)]
        )

    def rows_twice(values):
        count, rows = values.shape[:2]
        rows_buf[:count, pl.ds(0, rows, stride=2)] = values
        rows_buf[:count, pl.ds(1, rows, stride=2)] = values
        return rows_buf[:count, : 2 * rows]

    def coarse(values, lane_step):
        return row_pairs(pair_sum(pair_rows(values), lane_step, 2) * 0.125)

    def spread(values, step, axis):
        low = (iota(values.shape, axis) // step) % 2 == 0
        return (
            jnp.where(low, values, turn(values, step, axis)),
            jnp.where(low, turn(values, -step, axis), values),
        )

    def by_lane(values):
        lane = iota((8, 128), 1) % 4
        return jnp.where(
            lane < 2,
            jnp.where(lane == 0, values[0], values[1]),
            jnp.where(lane == 2, values[2], values[3]),
        )

    def twice_pair(values):
        return pair_sum(values, 1, 1)

    def gather(kind):
        for dx, dy in peers:
            rows = pl.ds(8 * ((ny - dy) % ny), 8)
            index = 2 * kind + (dx == 0)
            pltpu.make_async_remote_copy(
                src_ref=pack2.at[kind],
                dst_ref=grid2.at[kind, (nx - dx) % nx, rows],
                send_sem=spread_sem.at[0, index],
                recv_sem=spread_sem.at[1, index],
                device_id=at(dx, dy),
                device_id_type=MESH,
            ).start()
        grid2[kind, 0, :8] = pack2[kind]
        views = grid2.at[kind, pl.ds(1, nx - 1)], grid2.at[kind, 0, pl.ds(8, 8 * ny - 8)]
        return [
            pltpu.make_async_remote_copy(
                src_ref=view,
                dst_ref=view,
                send_sem=spread_sem.at[0, 2 * kind + index],
                recv_sem=spread_sem.at[1, 2 * kind + index],
                device_id=at(1 - index, index),
                device_id_type=MESH,
            )
            for index, view in enumerate(views)
        ]

    def drain(copies):
        for copy in copies:
            copy.wait_send()

    def swap1(kind, inner):
        first, rest = [], []
        edge1[kind, 0] = split_halves(whole1[kind, :4], whole1[kind, 4:], False, False)
        edge1[kind, 1] = split_halves(whole1[kind, :4], whole1[kind, 4:], True, True)

        def move(copies, src, dst, start, count, dx, dy, shift=0):
            if count > 0:
                source = src.at[pl.ds(start + shift, count)]
                copies.append(send(source, dst.at[pl.ds(start, count)], dx, dy))

        for copies in (first, rest):
            near = copies is first
            for side, dx in ((0, -1), (1, 1)):
                count = inner if near else HALO - inner
                start = 0 if (dx < 0) == near else HALO - count
                shift = 0 if dx < 0 else half - HALO
                move(copies, whole1.at[kind], from_x1.at[kind, side], start, count, dx, 0, shift)
            for place, (dx, dy) in enumerate(CORNERS):
                count = inner - 1 if near else HALO - inner
                if dx < 0:
                    start = 0 if near else inner - 1
                else:
                    start = HALO - inner + 1 if near else 1
                source = edge1.at[kind, (dy + 1) // 2]
                move(copies, source, from_d1.at[kind, place], start, count, dx, dy)
            if near:
                for side, dy in ((0, -1), (1, 1)):
                    copies.append(send(edge1.at[kind, side], from_y1.at[kind, side], 0, dy))
        return first, rest

    def padded1(kind, width):
        below, above = pl.ds(HALO - width + 1, width - 1), pl.ds(0, width - 1)
        lower = joined(from_d1[kind, 2, below], from_d1[kind, 3, below])[1]
        upper = joined(from_d1[kind, 0, above], from_d1[kind, 1, above])[0]
        center = jnp.concatenate(joined(from_y1[kind, 0], from_y1[kind, 1]), 0)
        inside = [from_x1[kind, 1, HALO - width :], whole1[kind], from_x1[kind, 0, :width]]
        return jnp.concatenate(
            [jnp.concatenate(inside, 0), halo_rows(center, lower, upper)], 1
        )

    def fields_of(start, inside, right, left):
        halos = joined(right, left)
        return tuple(
            Strip(start, jnp.concatenate([cells, halo], 1)) for cells, halo in zip(inside, halos)
        )

    def right_of_strip(conc):
        cells = conc.cells
        return conc, Strip(conc.start, cells * cells * cells - (1.0 + STABILIZER) * cells)

    mob1 = coarse(mobility_of(conc), 1)
    pack2[1] = by_lane(twice_pair(pair_sum(pair_rows(mob1), 2, 2) * 0.125))
    mob2_waits = gather(1)

    arrive(beside)
    level0 = Level(1.0, 1, 1, 2)
    middle = fields_of(0, (conc, chem), from_y0[0], from_y0[1])
    mob_middle = Strip(0, mobility_of(middle[0].cells))
    coupling, damp = level0.setup(mob_middle, 1, size - 1)
    right_middle = right_of_strip(middle[0])
    once_middle = level0.sweep(*middle, right_middle, 1, size - 1)
    both_middle = level0.sweep(*once_middle, right_middle, 2, size - 2)
    defect_middle = level0.residual(*both_middle, right_middle, 3, size - 3)

    arrive(outer)
    low_right = jnp.concatenate([from_d0[2][:1], from_d0[2]], 0)
    low_left = jnp.concatenate([from_d0[3][:1], from_d0[3]], 0)
    high_right = jnp.concatenate([from_d0[0], from_d0[0][-1:]], 0)
    high_left = jnp.concatenate([from_d0[1], from_d0[1][-1:]], 0)
    lows = fields_of(-HALO, (from_x0[1, 0], from_x0[1, 1]), low_right, low_left)
    highs = fields_of(size, (from_x0[0, 0], from_x0[0, 1]), high_right, high_left)
    fields = tuple(strips(*parts) for parts in zip(lows, middle, highs))
    mob_low, mob_high = (Strip(part[0].start, mobility_of(part[0].cells)) for part in (lows, highs))
    mob0 = strips(mob_low, mob_middle, mob_high)
    right_low, right_high = right_of_strip(lows[0]), right_of_strip(highs[0])
    right_side0 = tuple(strips(*parts) for parts in zip(right_low, right_middle, right_high))

    mob_x = pair_sum(pair_rows(mob0.at(-2, size + 2)), 1, 2) * 0.125
    mob1 = row_pairs(jnp.concatenate([mob_x, mob_x[:, 16:24]], 1))
    mob1_sum = near_sum(mob1, 1, 2)[:, :8]
    mob1 = mob1[1:-1, :8]
    even1 = iota((half, 8, 128), 2) % 2 == 0
    whole1[1] = jnp.where(even1, mob1, mob1_sum)
    mob1_waits, _ = swap1(1, HALO)

    coupling_low, damp_low = level0.setup(mob0, -3, 1)
    coupling_high, damp_high = level0.setup(mob0, size - 1, size + 3)
    level0.coupling = strips(coupling_low, coupling, coupling_high)
    level0.damp = strips(damp_low, damp, damp_high)

    def completed(now, before, low, high):
        inner = now[0].start, now[0].start + now[0].cells.shape[0]
        below = level0.sweep(*before, right_side0, low, inner[0])
        above = level0.sweep(*before, right_side0, inner[1], high)
        return tuple(strips(*parts) for parts in zip(below, now, above))

    once = completed(once_middle, fields, -3, size + 3)
    fields0 = completed(both_middle, once, -2, size + 2)
    below = level0.residual(*fields0, right_side0, 0, 3)
    above = level0.residual(*fields0, right_side0, size - 3, size)
    first, second = (
        jnp.concatenate(parts, 0)[:, :16] for parts in zip(below, defect_middle, above)
    )
    whole1[0] = jnp.where(even1, coarse(first, 1), coarse(second, 1))
    near_waits, far_waits = swap1(0, 2)

    arrive(mob1_waits)
    mob1, mob1_sum = spread(padded1(1, HALO), 1, 2)
    level1 = Level(0.25, 1, 2, 2)
    level1.setup(Strip(-HALO, mob1), -HALO, half + HALO, Strip(-HALO, mob1_sum))
    drain(outer + beside + mob1_waits)
    def by_row(values):
        zero, one = spread(values, 1, 2)
        zero, two = spread(zero, 2, 2)
        one, three = spread(one, 2, 2)
        together = jnp.stack([zero, one, two, three], 1)
        return together.reshape((nx * quarter,) + values.shape[1:])

    arrive(mob2_waits)
    mob2 = by_row(grid2[1, :, pl.ds(0, 4 * ny, stride=2)])
    mob3 = coarse(mob2, 4)
    level2, level3 = Level(0.0625, 1, 4, 4, True), Level(0.015625, 1, 8, 4, True)
    for level, mob in ((level2, mob2), (level3, mob3)):
        level.setup(wrapped(Strip(0, mob)), 0, mob.shape[0])

    drain(mob2_waits)
    arrive(near_waits)
    rhs1 = spread(padded1(0, 2), 1, 2)
    rhs1 = [Strip(-2, values) for values in rhs1]
    conc, chem = level1.step(rhs1, -2, half + 2)
    conc, chem = level1.sweep(conc, chem, rhs1, -1, half + 1)
    own = [
        twice_pair(pair_sum(pair_rows(values[:, :8]), 2, 2) * 0.125)
        for values in level1.residual(conc, chem, rhs1, 0, half)
    ]
    pack2[0] = jnp.where(iota((8, 128), 0) % 2 == 0, by_lane(own[0]), by_lane(own[1]))
    rhs2_waits = gather(0)

    arrive(far_waits)
    rhs1 = spread(padded1(0, HALO), 1, 2)
    rhs1 = [Strip(-HALO, values) for values in rhs1]
    conc, chem = level1.step(rhs1, -HALO, half + HALO)
    fields1 = level1.sweep(conc, chem, rhs1, -3, half + 3)

    drain(near_waits + far_waits)
    arrive(rhs2_waits)
    rhs2 = [by_row(grid2[0, :, pl.ds(start, 4 * ny, stride=2)]) for start in (0, 1)]
    rhs2 = [Strip(0, values) for values in rhs2]
    conc, chem = level2.step(rhs2, 0, nx * quarter)
    conc, chem = level2.sweep(conc, chem, rhs2, 0, nx * quarter)
    rhs3 = [coarse(v, 4) for v in level2.residual(conc, chem, rhs2, 0, nx * quarter)]
    rhs3 = [Strip(0, values) for values in rhs3]
    low_conc, low_chem = level3.step(rhs3, 0, nx * quarter // 2)
    low_conc, low_chem = level3.sweeps(COARSE - 1, low_conc, low_chem, rhs3)
    conc = Strip(0, conc.cells + twice(rows_twice(low_conc.cells)))
    chem = Strip(0, chem.cells + twice(rows_twice(low_chem.cells)))
    conc, chem = level2.sweeps(SWEEPS, conc, chem, rhs2)

    def around1(values):
        values = jnp.concatenate([values[-2:], values[: quarter + 2]], 0)
        values = rows_twice(values)
        low = iota((quarter + 4, 8, 128), 1) < 4
        beside = jnp.where(low, values[:, 8:16], values[:, -8:])
        return twice(jnp.concatenate([values[:, :8], beside], 1))[1:-1]

    conc, chem = (
        Strip(-3, old.cells + around1(new.cells)) for old, new in zip(fields1, (conc, chem))
    )
    conc, chem = level1.sweep(conc, chem, rhs1, -2, half + 2)
    conc, chem = level1.sweep(conc, chem, rhs1, -1, half + 1)

    def around0(values):
        doubled = rows_twice(values)
        low = iota((values.shape[0], 8, 128), 1) < 4
        beside = jnp.where(low, doubled[:, 16:24], doubled[:, 24:32])
        return twice(jnp.concatenate([doubled[:, :16], beside], 1))

    conc, chem = (
        Strip(-2, old.cells + around0(new.cells)) for old, new in zip(fields0, (conc, chem))
    )
    conc, chem = level0.sweep(conc, chem, right_side0, -1, size + 1)
    conc, chem = level0.sweep(conc, chem, right_side0, 0, size)
    result[0] = conc.cells[:, :16]
    result[1] = chem.cells[:, :16]
    drain(rhs2_waits)


def gathered_cycle(nx, ny, fields):
    size = fields.shape[1]
    half = size // 2
    copies = 8 + 8 + 14
    scratch = [
        (2, size, 8, 128),
        (2, 2, HALO, 16, 128),
        (2, size, 8, 128),
        (4, HALO - 1, 8, 128),
        (2, half, 8, 128),
        (2, 2, half // 2, 8, 128),
        (2, 2, HALO, 8, 128),
        (2, 2, half // 2, 8, 128),
        (2, 4, HALO, 8, 128),
        (2, 8, 128),
        (2, nx, ny * 8, 128),
        (2 * nx + half, 8 * ny, 128),
    ]
    shape = jax.ShapeDtypeStruct(fields.shape, jnp.float32)
    space = pl.BlockSpec(memory_space=pltpu.VMEM)
    return pl.pallas_call(
        functools.partial(cycle_kernel, nx, ny),
        out_shape=shape,
        in_specs=[space],
        out_specs=space,
        scratch_shapes=[pltpu.VMEM(dims, jnp.float32) for dims in scratch]
        + [pltpu.SemaphoreType.DMA((count,)) for count in (copies, copies)]
        + [pltpu.SemaphoreType.DMA((2, 4))],
        compiler_params=pltpu.CompilerParams(
            collective_id=0, has_side_effects=True, vmem_limit_bytes=32 * 1024 * 1024
        ),
    )(fields)


def body(conc_old, chem_old):
    nx, ny = lax.axis_size("gx"), lax.axis_size("gy")
    if conc_old.shape == (16, 16, 128) and nx >= 3 and ny == 4 and nx * ny <= 16:
        result = gathered_cycle(nx, ny, jnp.stack([conc_old, chem_old]))
    else:
        result = plain_solve(jnp.stack([conc_old, chem_old]))
    return (result[0], result[1])


def solution(mesh):
    in_specs = (P(("img", "gx"), "gy", None), P(("img", "gx"), "gy", None))
    out_specs = (P(("img", "gx"), "gy", None), P(("img", "gx"), "gy", None))
    return jax.shard_map(body, mesh=mesh, in_specs=in_specs, out_specs=out_specs, check_vma=False)
```

```python
import functools

import jax
import jax.numpy as jnp
from jax import lax
from jax.experimental import pallas as pl
from jax.experimental.pallas import tpu as pltpu
from jax.sharding import PartitionSpec as P

LEVELS = 4
SWEEPS = 2
COARSE = 6


TIME_STEP = 32.0
GRADIENT_ENERGY = 0.5
STABILIZER = 2.0
DAMPING = 0.7


def extended(cells, sides, width):
    for axis, dim in sides:
        count = lax.axis_size(axis)
        head = lax.slice_in_dim(cells, 0, width, axis=dim)
        tail = lax.slice_in_dim(cells, cells.shape[dim] - width, cells.shape[dim], axis=dim)
        cells = jnp.concatenate(
            [
                lax.ppermute(tail, axis, [(i, (i + 1) % count) for i in range(count)]),
                cells,
                lax.ppermute(head, axis, [((i + 1) % count, i) for i in range(count)]),
            ],
            axis=dim,
        )
    return cells


def mobility_of(concentration):
    return 0.1 + jnp.square(1.0 - concentration * concentration)


def right_of(concentration):
    return jnp.stack(
        [
            concentration,
            concentration * concentration * concentration - (1.0 + STABILIZER) * concentration,
        ]
    )


def face_weights(mob_padded, level_scale):
    middle = mob_padded[1:-1, 1:-1, :]
    half_scale = 0.5 * level_scale
    weights = (
        half_scale * (middle + mob_padded[2:, 1:-1, :]),
        half_scale * (middle + mob_padded[:-2, 1:-1, :]),
        half_scale * (middle + mob_padded[1:-1, 2:, :]),
        half_scale * (middle + mob_padded[1:-1, :-2, :]),
        half_scale * (middle + jnp.roll(middle, -1, axis=2)),
        half_scale * (middle + jnp.roll(middle, 1, axis=2)),
    )
    total_weight = weights[0] + weights[1] + weights[2] + weights[3] + weights[4] + weights[5]
    return (weights, total_weight)


def neighbour_list(padded, middle):
    return (
        padded[2:, 1:-1, :],
        padded[:-2, 1:-1, :],
        padded[1:-1, 2:, :],
        padded[1:-1, :-2, :],
        jnp.roll(middle, -1, axis=2),
        jnp.roll(middle, 1, axis=2),
    )


def apply_operator(padded, weights, level_scale):
    middle = padded[:, 1:-1, 1:-1, :]
    conc_near = neighbour_list(padded[0], middle[0])
    chem_near = neighbour_list(padded[1], middle[1])
    flux = weights[0] * (chem_near[0] - middle[1])
    for position in range(1, 6):
        flux = flux + weights[position] * (chem_near[position] - middle[1])
    laplace = (
        conc_near[0]
        + conc_near[1]
        + conc_near[2]
        + conc_near[3]
        + conc_near[4]
        + conc_near[5]
        - 6.0 * middle[0]
    )
    first_eq = middle[0] - TIME_STEP * flux
    second_eq = middle[1] - STABILIZER * middle[0] + GRADIENT_ENERGY * level_scale * laplace
    return jnp.stack([first_eq, second_eq])


def update(residual, total_weight, level_scale):
    diagonal = STABILIZER + 6.0 * GRADIENT_ENERGY * level_scale
    coupling = TIME_STEP * total_weight
    determinant = 1.0 + coupling * diagonal
    conc_step = (residual[0] - coupling * residual[1]) / determinant
    chem_step = (residual[1] + diagonal * residual[0]) / determinant
    return DAMPING * jnp.stack([conc_step, chem_step])


def sweep_once(padded, right_side, mob_padded, level_scale):
    weights, total_weight = face_weights(mob_padded, level_scale)
    residual = right_side - apply_operator(padded, weights, level_scale)
    return padded[:, 1:-1, 1:-1, :] + update(residual, total_weight, level_scale)


def defect(padded, right_side, mob_padded, level_scale):
    weights = face_weights(mob_padded, level_scale)[0]
    return right_side - apply_operator(padded, weights, level_scale)


def coarsen(values):
    dims_now = values.shape
    grouped = values.reshape(
        dims_now[:-3] + (dims_now[-3] // 2, 2, dims_now[-2] // 2, 2, dims_now[-1] // 2, 2)
    )
    return jnp.sum(grouped, axis=(-5, -3, -1)) * 0.125


def refine(values):
    for axis_pos in (-3, -2, -1):
        values = jnp.repeat(values, 2, axis=axis_pos)
    return values


def trim_rim(values, width):
    return values[..., width:-width, width:-width, :]


def field_rim(fields):
    return extended(fields, (("gx", 1), ("gy", 2)), 1)


def coarsest_solve(right_side, mobility, level_scale):
    mob_padded = extended(mobility, (("gx", 0), ("gy", 1)), 1)
    fields = update(right_side, face_weights(mob_padded, level_scale)[1], level_scale)
    for sweep_index in range(COARSE - 1):
        padded = extended(fields, (("gx", 1), ("gy", 2)), 1)
        fields = sweep_once(padded, right_side, mob_padded, level_scale)
    return fields


def plain_solve(start_fields):
    outer_fields = field_rim(start_fields)
    mob_outer = mobility_of(outer_fields[0])
    mobility = trim_rim(mob_outer, 1)
    level_data = []
    for level_index in range(LEVELS - 1):
        if level_index == 0:
            mob_padded = mob_outer
        else:
            mob_padded = extended(mobility, (("gx", 0), ("gy", 1)), 1)
        level_data.append((mob_padded, 0.25**level_index))
        mobility = coarsen(mobility)
    coarsest_scale = 0.25 ** (LEVELS - 1)

    def cycle_level(level_index, right_side):
        if level_index == LEVELS - 1:
            return coarsest_solve(right_side, mobility, coarsest_scale)
        mob_padded, level_scale = level_data[level_index]
        if level_index == 0:
            fields = sweep_once(outer_fields, right_side, mob_padded, level_scale)
        else:
            fields = update(right_side, face_weights(mob_padded, level_scale)[1], level_scale)
        fields = sweep_once(field_rim(fields), right_side, mob_padded, level_scale)
        residual = defect(field_rim(fields), right_side, mob_padded, level_scale)
        fields = fields + refine(cycle_level(level_index + 1, coarsen(residual)))
        for sweep_index in range(SWEEPS):
            fields = sweep_once(field_rim(fields), right_side, mob_padded, level_scale)
        return fields

    return cycle_level(0, right_of(start_fields[0]))


MESH = pl.DeviceIdType.MESH
HALO = 4
SIDES = (("lo", -1), ("hi", 1))
CORNERS = ((-1, -1), (-1, 1), (1, -1), (1, 1))


def iota(shape, dim):
    return lax.broadcasted_iota(jnp.int32, shape, dim)


def turn(values, shift, axis):
    size = values.shape[axis]
    return pltpu.roll(values, shift % size, axis)


def near_sum(values, row_step, lane_step):
    middle = values[1:-1]
    total = values[2:] + values[:-2]
    total = total + (turn(middle, row_step, 1) + turn(middle, -row_step, 1))
    return total + (turn(middle, lane_step, 2) + turn(middle, -lane_step, 2))


def pair_sum(values, step, axis):
    low = (iota(values.shape, axis) // step) % 2 == 0
    return values + jnp.where(low, turn(values, -step, axis), turn(values, step, axis))


def pair_rows(values):
    grouped = values.reshape((values.shape[0] // 2, 2) + values.shape[1:])
    return grouped[:, 0] + grouped[:, 1]


def twice(values):
    return jnp.concatenate([values[i // 2 : i // 2 + 1] for i in range(2 * values.shape[0])], 0)


class Strip:
    def __init__(self, start, cells):
        self.start, self.cells = start, cells

    def at(self, low, high):
        return self.cells[low - self.start : high - self.start]


def strips(*parts):
    return Strip(parts[0].start, jnp.concatenate([part.cells for part in parts], 0))


def wrapped(strip):
    cells = strip.cells
    return Strip(strip.start - 1, jnp.concatenate([cells[-1:], cells, cells[:1]], 0))


class Level:
    def __init__(self, scale, row_step, lane_step, layers, wrap=False):
        self.scale, self.layers = scale, layers
        self.row_step, self.lane_step, self.wrap = row_step, lane_step, wrap
        self.half = 0.5 * TIME_STEP * scale
        self.diagonal = STABILIZER + 6.0 * GRADIENT_ENERGY * scale
        self.mob = self.coupling = self.damp = None

    def pieces(self, work, low, high):
        parts = [
            work(at, min(at + self.layers, high)) for at in range(low, high, self.layers)
        ]
        return tuple(Strip(low, jnp.concatenate(cells, 0)) for cells in zip(*parts))

    def sums(self, values):
        return near_sum(values, self.row_step, self.lane_step)

    def setup(self, mob, low, high, mob_sum=None):
        def work(low, high):
            near = self.sums(mob.at(low - 1, high + 1)) if mob_sum is None else mob_sum.at(low, high)
            coupling = self.half * (6.0 * mob.at(low, high) + near)
            return coupling, DAMPING / (1.0 + coupling * self.diagonal)

        self.mob = mob
        self.coupling, self.damp = self.pieces(work, low, high)
        return self.coupling, self.damp

    def defect(self, conc, chem, right, low, high):
        c, u, mob = conc.at(low, high), chem.at(low, high), self.mob.at(low, high)
        near_chem = chem.at(low - 1, high + 1)
        carried = self.mob.at(low - 1, high + 1) * near_chem
        first = (
            right[0].at(low, high)
            - c
            + self.half * (mob * self.sums(near_chem) + self.sums(carried))
            - self.coupling.at(low, high) * u
        )
        near = self.sums(conc.at(low - 1, high + 1)) - 6.0 * c
        second = (
            right[1].at(low, high)
            - u
            + STABILIZER * c
            - (GRADIENT_ENERGY * self.scale) * near
        )
        return first, second

    def change(self, first, second, low, high):
        damp = self.damp.at(low, high)
        coupling = self.coupling.at(low, high)
        return damp * (first - coupling * second), damp * (second + self.diagonal * first)

    def residual(self, conc, chem, right, low, high):
        if self.wrap:
            conc, chem = wrapped(conc), wrapped(chem)
        parts = self.pieces(lambda *at: self.defect(conc, chem, right, *at), low, high)
        return tuple(part.cells for part in parts)

    def step(self, right, low, high):
        def work(low, high):
            return self.change(right[0].at(low, high), right[1].at(low, high), low, high)

        return self.pieces(work, low, high)

    def sweep(self, conc, chem, right, low, high):
        if self.wrap:
            conc, chem = wrapped(conc), wrapped(chem)

        def work(low, high):
            dc, du = self.change(*self.defect(conc, chem, right, low, high), low, high)
            return conc.at(low, high) + dc, chem.at(low, high) + du

        return self.pieces(work, low, high)

    def sweeps(self, count, conc, chem, right):
        size = conc.cells.shape[0]

        def once(_, now):
            new = self.sweep(Strip(0, now[0]), Strip(0, now[1]), right, 0, size)
            return new[0].cells, new[1].cells

        now = lax.fori_loop(0, count, once, (conc.cells, chem.cells))
        return Strip(0, now[0]), Strip(0, now[1])


def split_halves(first, second, first_high, second_high):
    low = iota(first.shape, 1) < 4
    first = turn(first, 4, 1) if first_high else first
    second = second if second_high else turn(second, 4, 1)
    return jnp.where(low, first, second)


def cycle_kernel(nx, ny, own, result, *scratch):
    (
        edge0,
        from_x0,
        from_y0,
        from_d0,
        whole1,
        edge1,
        from_x1,
        from_y1,
        from_d1,
        pack2,
        grid2,
        rows_buf,
        send_sem,
        recv_sem,
        spread_sem,
    ) = scratch
    img, gx, gy = lax.axis_index("img"), lax.axis_index("gx"), lax.axis_index("gy")
    x_at = [lax.rem(gx + dx, nx) for dx in range(nx)]
    y_at = [lax.rem(gy + dy, ny) for dy in range(ny)]

    def at(dx, dy):
        return (img, x_at[dx % nx], y_at[dy % ny])

    peers = [(dx, dy) for dx in [*range(1, nx), 0] for dy in range(ny) if (dx, dy) != (0, 0)]
    barrier = pltpu.get_barrier_semaphore()
    for dx, dy in peers:
        pl.semaphore_signal(barrier, inc=1, device_id=at(dx, dy), device_id_type=MESH)

    used = [0]

    def send(src, dst, dx, dy):
        index = used[0]
        used[0] += 1
        copy = pltpu.make_async_remote_copy(
            src_ref=src,
            dst_ref=dst,
            send_sem=send_sem.at[index],
            recv_sem=recv_sem.at[index],
            device_id=at(dx, dy),
            device_id_type=MESH,
        )
        copy.start()
        return copy

    def arrive(copies):
        for copy in copies:
            copy.wait_recv()

    size = own.shape[1]
    half = size // 2
    quarter = half // 2
    conc, chem = own[0], own[1]
    edge0[0] = split_halves(conc[:, :8], chem[:, :8], False, False)
    edge0[1] = split_halves(conc[:, -8:], chem[:, -8:], True, True)
    pl.semaphore_wait(barrier, len(peers))

    outer, beside = [], []
    for side, dx in ((0, -1), (1, 1)):
        rows = pl.ds(0, HALO) if dx < 0 else pl.ds(size - HALO, HALO)
        outer.append(send(own.at[:, rows], from_x0.at[side], dx, 0))
    for side, dy in ((0, -1), (1, 1)):
        beside.append(send(edge0.at[side], from_y0.at[side], 0, dy))
    for place, (dx, dy) in enumerate(CORNERS):
        rows = pl.ds(0, HALO - 1) if dx < 0 else pl.ds(size - HALO + 1, HALO - 1)
        outer.append(send(edge0.at[(dy + 1) // 2, rows], from_d0.at[place], dx, dy))

    def halo_rows(center, lower, upper):
        return jnp.concatenate([lower[:1], lower, center, upper, upper[-1:]], 0)

    def joined(right, left):
        low = iota(right.shape, 1) < 4
        return jnp.where(low, right, turn(left, 4, 1)), jnp.where(low, turn(right, 4, 1), left)

    def row_pairs(values):
        count, rows = values.shape[:2]
        rows_buf[:count, :rows] = values
        return (
            rows_buf[:count, pl.ds(0, rows // 2, stride=2)]
            + rows_buf[:count, pl.ds(1, rows // 2, stride=2)]
        )

    def rows_twice(values):
        count, rows = values.shape[:2]
        rows_buf[:count, pl.ds(0, rows, stride=2)] = values
        rows_buf[:count, pl.ds(1, rows, stride=2)] = values
        return rows_buf[:count, : 2 * rows]

    def coarse(values, lane_step):
        return row_pairs(pair_sum(pair_rows(values), lane_step, 2) * 0.125)

    def spread(values, step, axis):
        low = (iota(values.shape, axis) // step) % 2 == 0
        return (
            jnp.where(low, values, turn(values, step, axis)),
            jnp.where(low, turn(values, -step, axis), values),
        )

    def by_lane(values):
        lane = iota((8, 128), 1) % 4
        return jnp.where(
            lane < 2,
            jnp.where(lane == 0, values[0], values[1]),
            jnp.where(lane == 2, values[2], values[3]),
        )

    def twice_pair(values):
        return pair_sum(values, 1, 1)

    def gather(kind):
        for dx, dy in peers:
            rows = pl.ds(8 * ((ny - dy) % ny), 8)
            index = 2 * kind + (dx == 0)
            pltpu.make_async_remote_copy(
                src_ref=pack2.at[kind],
                dst_ref=grid2.at[kind, (nx - dx) % nx, rows],
                send_sem=spread_sem.at[0, index],
                recv_sem=spread_sem.at[1, index],
                device_id=at(dx, dy),
                device_id_type=MESH,
            ).start()
        grid2[kind, 0, :8] = pack2[kind]
        views = grid2.at[kind, pl.ds(1, nx - 1)], grid2.at[kind, 0, pl.ds(8, 8 * ny - 8)]
        return [
            pltpu.make_async_remote_copy(
                src_ref=view,
                dst_ref=view,
                send_sem=spread_sem.at[0, 2 * kind + index],
                recv_sem=spread_sem.at[1, 2 * kind + index],
                device_id=at(1 - index, index),
                device_id_type=MESH,
            )
            for index, view in enumerate(views)
        ]

    def drain(copies):
        for copy in copies:
            copy.wait_send()

    def swap1(kind, inner):
        first, rest = [], []
        edge1[kind, 0] = split_halves(whole1[kind, :4], whole1[kind, 4:], False, False)
        edge1[kind, 1] = split_halves(whole1[kind, :4], whole1[kind, 4:], True, True)

        def move(copies, src, dst, start, count, dx, dy, shift=0):
            if count > 0:
                source = src.at[pl.ds(start + shift, count)]
                copies.append(send(source, dst.at[pl.ds(start, count)], dx, dy))

        for copies in (first, rest):
            near = copies is first
            for side, dx in ((0, -1), (1, 1)):
                count = inner if near else HALO - inner
                start = 0 if (dx < 0) == near else HALO - count
                shift = 0 if dx < 0 else half - HALO
                move(copies, whole1.at[kind], from_x1.at[kind, side], start, count, dx, 0, shift)
            for place, (dx, dy) in enumerate(CORNERS):
                count = inner - 1 if near else HALO - inner
                if dx < 0:
                    start = 0 if near else inner - 1
                else:
                    start = HALO - inner + 1 if near else 1
                source = edge1.at[kind, (dy + 1) // 2]
                move(copies, source, from_d1.at[kind, place], start, count, dx, dy)
            if near:
                for side, dy in ((0, -1), (1, 1)):
                    copies.append(send(edge1.at[kind, side], from_y1.at[kind, side], 0, dy))
        return first, rest

    def padded1(kind, width):
        below, above = pl.ds(HALO - width + 1, width - 1), pl.ds(0, width - 1)
        lower = joined(from_d1[kind, 2, below], from_d1[kind, 3, below])[1]
        upper = joined(from_d1[kind, 0, above], from_d1[kind, 1, above])[0]
        center = jnp.concatenate(joined(from_y1[kind, 0], from_y1[kind, 1]), 0)
        inside = [from_x1[kind, 1, HALO - width :], whole1[kind], from_x1[kind, 0, :width]]
        return jnp.concatenate(
            [jnp.concatenate(inside, 0), halo_rows(center, lower, upper)], 1
        )

    def fields_of(start, inside, right, left):
        halos = joined(right, left)
        return tuple(
            Strip(start, jnp.concatenate([cells, halo], 1)) for cells, halo in zip(inside, halos)
        )

    def right_of_strip(conc):
        cells = conc.cells
        return conc, Strip(conc.start, cells * cells * cells - (1.0 + STABILIZER) * cells)

    arrive(beside)
    level0 = Level(1.0, 1, 1, 2)
    middle = fields_of(0, (conc, chem), from_y0[0], from_y0[1])
    mob_middle = Strip(0, mobility_of(middle[0].cells))
    coupling, damp = level0.setup(mob_middle, 1, size - 1)
    right_middle = right_of_strip(middle[0])
    once_middle = level0.sweep(*middle, right_middle, 1, size - 1)
    both_middle = level0.sweep(*once_middle, right_middle, 2, size - 2)
    defect_middle = level0.residual(*both_middle, right_middle, 3, size - 3)

    arrive(outer)
    low_right = jnp.concatenate([from_d0[2][:1], from_d0[2]], 0)
    low_left = jnp.concatenate([from_d0[3][:1], from_d0[3]], 0)
    high_right = jnp.concatenate([from_d0[0], from_d0[0][-1:]], 0)
    high_left = jnp.concatenate([from_d0[1], from_d0[1][-1:]], 0)
    lows = fields_of(-HALO, (from_x0[1, 0], from_x0[1, 1]), low_right, low_left)
    highs = fields_of(size, (from_x0[0, 0], from_x0[0, 1]), high_right, high_left)
    fields = tuple(strips(*parts) for parts in zip(lows, middle, highs))
    mob_low, mob_high = (Strip(part[0].start, mobility_of(part[0].cells)) for part in (lows, highs))
    mob0 = strips(mob_low, mob_middle, mob_high)
    right_low, right_high = right_of_strip(lows[0]), right_of_strip(highs[0])
    right_side0 = tuple(strips(*parts) for parts in zip(right_low, right_middle, right_high))

    mob_x = pair_sum(pair_rows(mob0.at(-2, size + 2)), 1, 2) * 0.125
    mob1 = row_pairs(jnp.concatenate([mob_x, mob_x[:, 16:24]], 1))
    mob1_sum = near_sum(mob1, 1, 2)[:, :8]
    mob1 = mob1[1:-1, :8]
    even1 = iota((half, 8, 128), 2) % 2 == 0
    whole1[1] = jnp.where(even1, mob1, mob1_sum)
    mob1_waits, _ = swap1(1, HALO)
    pack2[1] = by_lane(twice_pair(pair_sum(pair_rows(mob1), 2, 2) * 0.125))

    coupling_low, damp_low = level0.setup(mob0, -3, 1)
    coupling_high, damp_high = level0.setup(mob0, size - 1, size + 3)
    level0.coupling = strips(coupling_low, coupling, coupling_high)
    level0.damp = strips(damp_low, damp, damp_high)

    def completed(now, before, low, high):
        inner = now[0].start, now[0].start + now[0].cells.shape[0]
        below = level0.sweep(*before, right_side0, low, inner[0])
        above = level0.sweep(*before, right_side0, inner[1], high)
        return tuple(strips(*parts) for parts in zip(below, now, above))

    once = completed(once_middle, fields, -3, size + 3)
    fields0 = completed(both_middle, once, -2, size + 2)
    below = level0.residual(*fields0, right_side0, 0, 3)
    above = level0.residual(*fields0, right_side0, size - 3, size)
    first, second = (
        jnp.concatenate(parts, 0)[:, :16] for parts in zip(below, defect_middle, above)
    )
    whole1[0] = jnp.where(even1, coarse(first, 1), coarse(second, 1))
    near_waits, far_waits = swap1(0, 2)
    mob2_waits = gather(1)

    arrive(mob1_waits)
    mob1, mob1_sum = spread(padded1(1, HALO), 1, 2)
    level1 = Level(0.25, 1, 2, 2)
    level1.setup(Strip(-HALO, mob1), -HALO, half + HALO, Strip(-HALO, mob1_sum))
    drain(outer + beside + mob1_waits)
    arrive(near_waits)
    rhs1 = spread(padded1(0, 2), 1, 2)
    rhs1 = [Strip(-2, values) for values in rhs1]
    conc, chem = level1.step(rhs1, -2, half + 2)
    conc, chem = level1.sweep(conc, chem, rhs1, -1, half + 1)
    own = [
        twice_pair(pair_sum(pair_rows(values[:, :8]), 2, 2) * 0.125)
        for values in level1.residual(conc, chem, rhs1, 0, half)
    ]
    pack2[0] = jnp.where(iota((8, 128), 0) % 2 == 0, by_lane(own[0]), by_lane(own[1]))
    rhs2_waits = gather(0)

    arrive(far_waits)
    rhs1 = spread(padded1(0, HALO), 1, 2)
    rhs1 = [Strip(-HALO, values) for values in rhs1]
    conc, chem = level1.step(rhs1, -HALO, half + HALO)
    fields1 = level1.sweep(conc, chem, rhs1, -3, half + 3)

    def by_row(values):
        zero, one = spread(values, 1, 2)
        zero, two = spread(zero, 2, 2)
        one, three = spread(one, 2, 2)
        together = jnp.stack([zero, one, two, three], 1)
        return together.reshape((nx * quarter,) + values.shape[1:])

    arrive(mob2_waits)
    mob2 = by_row(grid2[1, :, pl.ds(0, 4 * ny, stride=2)])
    mob3 = coarse(mob2, 4)
    level2, level3 = Level(0.0625, 1, 4, 4, True), Level(0.015625, 1, 8, 4, True)
    for level, mob in ((level2, mob2), (level3, mob3)):
        level.setup(wrapped(Strip(0, mob)), 0, mob.shape[0])

    drain(near_waits + far_waits + mob2_waits)
    arrive(rhs2_waits)
    rhs2 = [by_row(grid2[0, :, pl.ds(start, 4 * ny, stride=2)]) for start in (0, 1)]
    rhs2 = [Strip(0, values) for values in rhs2]
    conc, chem = level2.step(rhs2, 0, nx * quarter)
    conc, chem = level2.sweep(conc, chem, rhs2, 0, nx * quarter)
    rhs3 = [coarse(v, 4) for v in level2.residual(conc, chem, rhs2, 0, nx * quarter)]
    rhs3 = [Strip(0, values) for values in rhs3]
    low_conc, low_chem = level3.step(rhs3, 0, nx * quarter // 2)
    low_conc, low_chem = level3.sweeps(COARSE - 1, low_conc, low_chem, rhs3)
    conc = Strip(0, conc.cells + twice(rows_twice(low_conc.cells)))
    chem = Strip(0, chem.cells + twice(rows_twice(low_chem.cells)))
    conc, chem = level2.sweeps(SWEEPS, conc, chem, rhs2)

    def around1(values):
        values = jnp.concatenate([values[-2:], values[: quarter + 2]], 0)
        values = rows_twice(values)
        low = iota((quarter + 4, 8, 128), 1) < 4
        beside = jnp.where(low, values[:, 8:16], values[:, -8:])
        return twice(jnp.concatenate([values[:, :8], beside], 1))[1:-1]

    conc, chem = (
        Strip(-3, old.cells + around1(new.cells)) for old, new in zip(fields1, (conc, chem))
    )
    conc, chem = level1.sweep(conc, chem, rhs1, -2, half + 2)
    conc, chem = level1.sweep(conc, chem, rhs1, -1, half + 1)

    def around0(values):
        doubled = rows_twice(values)
        low = iota((values.shape[0], 8, 128), 1) < 4
        beside = jnp.where(low, doubled[:, 16:24], doubled[:, 24:32])
        return twice(jnp.concatenate([doubled[:, :16], beside], 1))

    conc, chem = (
        Strip(-2, old.cells + around0(new.cells)) for old, new in zip(fields0, (conc, chem))
    )
    conc, chem = level0.sweep(conc, chem, right_side0, -1, size + 1)
    conc, chem = level0.sweep(conc, chem, right_side0, 0, size)
    result[0] = conc.cells[:, :16]
    result[1] = chem.cells[:, :16]
    drain(rhs2_waits)


def gathered_cycle(nx, ny, fields):
    size = fields.shape[1]
    half = size // 2
    copies = 8 + 8 + 14
    scratch = [
        (2, size, 8, 128),
        (2, 2, HALO, 16, 128),
        (2, size, 8, 128),
        (4, HALO - 1, 8, 128),
        (2, half, 8, 128),
        (2, 2, half // 2, 8, 128),
        (2, 2, HALO, 8, 128),
        (2, 2, half // 2, 8, 128),
        (2, 4, HALO, 8, 128),
        (2, 8, 128),
        (2, nx, ny * 8, 128),
        (2 * nx + half, 8 * ny, 128),
    ]
    shape = jax.ShapeDtypeStruct(fields.shape, jnp.float32)
    space = pl.BlockSpec(memory_space=pltpu.VMEM)
    return pl.pallas_call(
        functools.partial(cycle_kernel, nx, ny),
        out_shape=shape,
        in_specs=[space],
        out_specs=space,
        scratch_shapes=[pltpu.VMEM(dims, jnp.float32) for dims in scratch]
        + [pltpu.SemaphoreType.DMA((count,)) for count in (copies, copies)]
        + [pltpu.SemaphoreType.DMA((2, 4))],
        compiler_params=pltpu.CompilerParams(
            collective_id=0, has_side_effects=True, vmem_limit_bytes=32 * 1024 * 1024
        ),
    )(fields)


def body(conc_old, chem_old):
    nx, ny = lax.axis_size("gx"), lax.axis_size("gy")
    if conc_old.shape == (16, 16, 128) and nx >= 3 and ny == 4 and nx * ny <= 16:
        result = gathered_cycle(nx, ny, jnp.stack([conc_old, chem_old]))
    else:
        result = plain_solve(jnp.stack([conc_old, chem_old]))
    return (result[0], result[1])


def solution(mesh):
    in_specs = (P(("img", "gx"), "gy", None), P(("img", "gx"), "gy", None))
    out_specs = (P(("img", "gx"), "gy", None), P(("img", "gx"), "gy", None))
    return jax.shard_map(body, mesh=mesh, in_specs=in_specs, out_specs=out_specs, check_vma=False)
```
